32 devices in a mesh: proj: 8 (over y, x, core), tile: 4 (over z).
Axes of the slice: x: 2, y: 2, z: 4, core: 2. Of those that a mesh axis runs over, the one named last changes fastest.
Arguments:
- raw: bfloat16 [16, 1024, 4096], P(None, 'proj', 'tile'), may hold values from -6 to 6
- row_weights: bfloat16 [16, 4, 128, 256], P('proj', 'tile'), may hold values from 0 to 1
- col_weights: bfloat16 [16, 4, 1024, 2048], P('proj', 'tile'), may hold values from 0 to 1
- band_start: int32 [16, 4], replicated, may hold values from 0 to 768
- band_length: int32 [16, 4], replicated, may hold values from 64 to 256, as said below
- col_offset: int32 [16, 4], P('proj', 'tile'), may hold values from 0 to 24
Outputs:
- slab: float32 [128, 8192], P('proj', 'tile')
The draws below stay inside these ranges and needn't reach their ends.
Inputs may be any that keep to these rules, and one draw needn't show every extreme that they name: `band_length`: in every projection some tile uses exactly 256 rows.
All inputs are finite; a program needn't handle non-finite values.
Results may differ from the reference program's by a relative error of at most 0.008.
Values may be sent and summed in bfloat16 or wider, within the bound.
A program may use at most 128 MiB of HBM per device.

```python
import math
import jax
import jax.numpy as jnp
from jax import lax

DU = 4096
BAND = 1024
LMAX = 256
CW = 1024
SLICES = 128
VT = 2048
P_SIZE = 16
TILES = 4


def draw_band_length(key, part):
    key = jax.random.fold_in(key, 11)
    first, second = jax.random.split(key)
    base = jax.random.randint(first, (P_SIZE, TILES), LMAX // 4, LMAX + 1)
    pick = jax.random.randint(second, (P_SIZE,), 0, TILES)
    full = jnp.arange(TILES, dtype=jnp.int32)[None, :] == pick[:, None]
    return jnp.where(full, LMAX, base).astype(jnp.int32)


def draw_row_weights(key, part):
    key = jax.random.fold_in(key, 21)
    first, second = jax.random.split(key)
    jitter = jax.random.uniform(first, (P_SIZE, TILES, 1, 1), jnp.float32, -LMAX / 8.0, LMAX / 8.0)
    center = (jnp.arange(SLICES, dtype=jnp.float32) + 0.5)[None, None, :, None] * (LMAX / SLICES) + jitter
    gap = jnp.abs(jnp.arange(LMAX, dtype=jnp.float32)[None, None, None, :] - center)
    spread_width = 2.0
    hat = jnp.maximum(0.0, 1.0 - gap / spread_width) / spread_width
    rough = jax.random.uniform(second, (P_SIZE, TILES, SLICES, LMAX), jnp.float32, 0.5, 1.5)
    return (hat * rough).astype(jnp.bfloat16)


def draw_col_weights(key, part):
    key = jax.random.fold_in(key, 31)
    first, second = jax.random.split(key)
    jitter = jax.random.uniform(first, (P_SIZE, TILES, 1, 1), jnp.float32, -CW / 16.0, CW / 16.0)
    center = (jnp.arange(VT, dtype=jnp.float32) + 0.5)[None, None, None, :] * (CW / VT) + jitter
    gap = jnp.abs(jnp.arange(CW, dtype=jnp.float32)[None, None, :, None] - center)
    spread_width = max(2.0, 2.0 * CW / VT)
    hat = jnp.maximum(0.0, 1.0 - gap / spread_width) / spread_width
    rough = jax.random.uniform(second, (P_SIZE, TILES, CW, VT), jnp.float32, 0.5, 1.5)
    return (hat * rough).astype(jnp.bfloat16)


def touch_ends(array, key, least, top_value):
    longest = array.shape.index(max(array.shape))
    spots = []
    for shift in (0, 1):
        where = [jax.random.randint(jax.random.fold_in(key, axis), (), 0, length) for axis, length in enumerate(array.shape)]
        where[longest] = (where[longest] + shift) % array.shape[longest]
        spots.append(tuple(where))
    return array.at[spots[0]].set(least).at[spots[1]].set(top_value)


def block_scale(key, shape, cuts, smallest, top_value):
    loudness, own = 1.0, jax.random.fold_in(key, 6)
    for axis_at, blocks in cuts:
        draws = jnp.exp(jax.random.uniform(jax.random.fold_in(own, axis_at), (blocks,), jnp.float32, smallest / len(cuts), top_value / len(cuts)))
        loudness = loudness * jnp.repeat(draws, shape[axis_at] // blocks).reshape([-1 if axis == axis_at else 1 for axis in range(len(shape))])
    return loudness


def noise(key, dims, scale, reach, pieces=(), held_as=jnp.bfloat16):
    factor_of = block_scale(key, dims, pieces, -0.22, 0.18) if pieces else 1.0
    array = jax.random.normal(key, dims, jnp.float32) * scale * factor_of
    return jnp.minimum(jnp.maximum(array, -reach), reach).astype(held_as)


def setup_inputs(seed: int = 0) -> dict:
    streams_of = jax.random.split(jax.random.key(seed), 7)
    return {
        "raw": noise(streams_of[0], (P_SIZE, BAND, DU), 1.0, 6.0, ((1, 8), (2, 4))),
        "row_weights": draw_row_weights(jax.random.fold_in(streams_of[6], 71), 0),
        "col_weights": draw_col_weights(jax.random.fold_in(streams_of[6], 71), 0),
        "band_start": touch_ends(jax.random.randint(streams_of[3], (P_SIZE, TILES), 0, BAND - LMAX + 1), jax.random.fold_in(streams_of[3], 1), 0, BAND - LMAX).astype(jnp.int32),
        "band_length": draw_band_length(jax.random.fold_in(streams_of[6], 71), 0),
        "col_offset": touch_ends(jax.random.randint(streams_of[5], (P_SIZE, TILES), 0, DU // 128 - CW // 128 + 1), jax.random.fold_in(streams_of[5], 1), 0, (DU // 128 - CW // 128 + 1) - 1).astype(jnp.int32),
    }


def tap_tiles():
    rows_a = jnp.arange(128, dtype=jnp.int32)[:, None]
    cols_c = jnp.arange(128, dtype=jnp.int32)[None, :]
    tiles = []
    for shift in (-1, 0, 1):
        offset = cols_c - rows_a - 128 * shift
        offset_f = offset.astype(jnp.float32)
        odd_mask = offset % 2 != 0
        safe_sq = jnp.where(offset == 0, 1.0, offset_f * offset_f)
        value = jnp.where(offset == 0, 0.25, jnp.where(odd_mask, -1.0 / (math.pi * math.pi * safe_sq), 0.0))
        value = jnp.where((offset >= -128) & (offset <= 127), value, 0.0)
        tiles.append(value.astype(jnp.bfloat16))
    return tiles

def cos_weight(rows, cols, total_rows, total_cols):
    dist = 2.0 * total_cols
    vcoord = rows.astype(jnp.float32) + 0.5 - total_rows / 2.0
    ucoord = cols.astype(jnp.float32) + 0.5 - total_cols / 2.0
    return dist / jnp.sqrt(dist * dist + ucoord[None, :] ** 2 + vcoord[:, None] ** 2)

def filter_one(proj_rows, tiles):
    rows_n, cols_n = proj_rows.shape
    weight = cos_weight(jnp.arange(rows_n, dtype=jnp.int32), jnp.arange(cols_n, dtype=jnp.int32), rows_n, cols_n)
    weighted = (proj_rows.astype(jnp.float32) * weight).astype(jnp.bfloat16)
    padded = jnp.pad(weighted, ((0, 0), (128, 128)))
    total = jnp.zeros((rows_n, cols_n // 128, 128), jnp.float32)
    for index in range(3):
        piece = padded[:, 128 * index:128 * index + cols_n].reshape(rows_n, cols_n // 128, 128)
        total = total + jnp.einsum('rna,ab->rnb', piece.astype(jnp.float32), tiles[index].astype(jnp.float32), precision=lax.Precision.HIGHEST)
    return total.reshape(rows_n, cols_n).astype(jnp.bfloat16)

def reference(raw, row_weights, col_weights, band_start, band_length, col_offset):
    tiles = tap_tiles()
    filtered = lax.map(lambda x: filter_one(x, tiles), raw)

    def one_pair(proj_data, rw, cw, start, length, offset):
        rows = lax.dynamic_slice_in_dim(proj_data, start, LMAX, 0)
        mask = jnp.arange(LMAX, dtype=jnp.int32)[:, None] < length
        rows = jnp.where(mask, rows, jnp.zeros_like(rows))
        window = lax.dynamic_slice_in_dim(rows, offset * 128, CW, 1)
        spread = jnp.dot(window.astype(jnp.float32), cw.astype(jnp.float32), precision=lax.Precision.HIGHEST).astype(jnp.bfloat16)
        return jnp.dot(rw.astype(jnp.float32), spread.astype(jnp.float32), precision=lax.Precision.HIGHEST)

    def step(acc, items):
        proj_data, rw, cw, start, length, offset = items
        terms = jax.vmap(one_pair, in_axes=(None, 0, 0, 0, 0, 0))(proj_data, rw, cw, start, length, offset)
        return (acc + terms, None)
    init = jnp.zeros((TILES, SLICES, VT), jnp.float32)
    acc, _ = lax.scan(step, init, (filtered, row_weights, col_weights, band_start, band_length, col_offset))
    return jnp.transpose(acc, (1, 0, 2)).reshape(SLICES, TILES * VT)
```

```python
import math

import jax
import jax.numpy as jnp
from jax import lax
from jax.sharding import PartitionSpec as P


def tap_tiles():
    rows_a = jnp.arange(128, dtype=jnp.int32)[:, None]
    cols_c = jnp.arange(128, dtype=jnp.int32)[None, :]
    tiles = []
    for shift in (-1, 0, 1):
        offset = cols_c - rows_a - 128 * shift
        offset_f = offset.astype(jnp.float32)
        odd_mask = offset % 2 != 0
        safe_sq = jnp.where(offset == 0, 1.0, offset_f * offset_f)
        value = jnp.where(
            offset == 0, 0.25, jnp.where(odd_mask, -1.0 / (math.pi * math.pi * safe_sq), 0.0)
        )
        value = jnp.where((offset >= -128) & (offset <= 127), value, 0.0)
        tiles.append(value.astype(jnp.bfloat16))
    return tiles


def banded_rows(weights, starts, lengths, total_rows):
    lmax = weights.shape[-1]
    keep = jnp.arange(lmax, dtype=jnp.int32) < lengths[..., None]
    weights = jnp.where(keep[:, :, None, :], weights, jnp.zeros_like(weights))

    def place(w, start):
        wide = jnp.zeros((w.shape[0], total_rows), w.dtype)
        return lax.dynamic_update_slice(wide, w, (0, start))

    return jax.vmap(jax.vmap(place))(weights, starts)


def body(raw, row_weights, col_weights, band_start, band_length, col_offset):
    proj_count, rows_dev, cols_dev = raw.shape
    n_proj = lax.axis_size("proj")
    n_tile = lax.axis_size("tile")
    proj_me = lax.axis_index("proj")
    tile_me = lax.axis_index("tile")
    total_rows = rows_dev * n_proj
    total_cols = cols_dev * n_tile
    local_count = proj_count // n_proj
    slices = row_weights.shape[2]
    win_cols = col_weights.shape[2]
    dist = 2.0 * total_cols

    first_proj = proj_me * local_count
    starts = lax.dynamic_slice_in_dim(band_start, first_proj, local_count, 0)
    lengths = lax.dynamic_slice_in_dim(band_length, first_proj, local_count, 0)
    all_rw = lax.all_gather(row_weights, "tile", axis=1, tiled=True)
    wide = banded_rows(all_rw, starts, lengths, total_rows)
    wide = wide.reshape(local_count, n_tile * slices, total_rows)

    owned = lax.all_to_all(raw, "proj", split_axis=0, concat_axis=1, tiled=True)
    row_ids = jnp.arange(total_rows, dtype=jnp.int32).astype(jnp.float32)
    col_ids = (tile_me * cols_dev + jnp.arange(cols_dev, dtype=jnp.int32)).astype(jnp.float32)
    vcoord = row_ids + 0.5 - total_rows / 2.0
    ucoord = col_ids + 0.5 - total_cols / 2.0
    weight = dist / jnp.sqrt(dist * dist + ucoord[None, :] ** 2 + vcoord[:, None] ** 2)
    weighted = (owned.astype(jnp.float32) * weight[None]).astype(jnp.bfloat16)

    mixed = jnp.einsum("psr,prc->psc", wide, weighted, preferred_element_type=jnp.float32)
    mixed = mixed.astype(jnp.bfloat16).reshape(local_count, n_tile, slices, cols_dev)
    mine = lax.all_to_all(mixed, "tile", split_axis=1, concat_axis=3, tiled=True)
    mine = jnp.pad(mine[:, 0], ((0, 0), (0, 0), (128, 128)))
    blocks = win_cols // 128
    tiles = tap_tiles()
    windows = []
    for local in range(local_count):
        part = lax.dynamic_slice_in_dim(
            mine[local], 128 * col_offset[local, 0], win_cols + 256, 1
        )
        total = jnp.zeros((slices, blocks, 128), jnp.float32)
        for index in range(3):
            piece = part[:, 128 * index : 128 * index + win_cols].reshape(slices, blocks, 128)
            total = total + jnp.einsum(
                "rna,ab->rnb", piece, tiles[index], preferred_element_type=jnp.float32
            )
        windows.append(total.reshape(slices, win_cols).astype(jnp.bfloat16))
    acc = jnp.zeros((slices, col_weights.shape[3]), jnp.float32)
    for local in range(local_count):
        acc = acc + jnp.dot(
            windows[local], col_weights[local, 0], preferred_element_type=jnp.float32
        )
    parts = acc.astype(jnp.bfloat16).reshape(n_proj, slices // n_proj, -1)
    parts = lax.all_to_all(parts, "proj", split_axis=0, concat_axis=0, tiled=True)
    return jnp.sum(parts.astype(jnp.float32), axis=0)


def solution(mesh):
    return jax.shard_map(
        body,
        mesh=mesh,
        in_specs=(
            P(None, "proj", "tile"),
            P("proj", "tile", None, None),
            P("proj", "tile", None, None),
            P(),
            P(),
            P("proj", "tile"),
        ),
        out_specs=P("proj", "tile"),
        check_vma=False,
    )
```

```python
import functools
import math

import jax
import jax.numpy as jnp
import ml_dtypes
import numpy as np
from jax import lax
from jax.experimental import pallas as pl
from jax.experimental.pallas import tpu as pltpu
from jax.sharding import PartitionSpec as P

MESH = pl.DeviceIdType.MESH
CHUNK = 256
PARTS = 2


def tap_matrix():
    n = np.arange(256)[None, :] - np.arange(512)[:, None] + 128
    n_f = np.where(n == 0, 1, n).astype(np.float32)
    odd = -np.float32(1.0) / (np.float32(math.pi * math.pi) * (n_f * n_f))
    value = np.where(n == 0, np.float32(0.25), np.where(n % 2 != 0, odd, np.float32(0.0)))
    value = np.where((n >= -128) & (n <= 127), value, np.float32(0.0))
    return value.astype(ml_dtypes.bfloat16)


def kernel(
    n_proj, n_tile, chunks, cw,
    starts, lengths, offsets, taps, rw, raw, col_w, out,
    landing, wide, weighted, ybuf, zbuf, rwland, filt, cbuf, psend, precv,
    own_sem, raw_send, raw_recv, rw_send, rw_recv, z_send, z_recv, c_sem, p_send, p_recv,
):
    me_p = lax.axis_index("proj")
    me_t = lax.axis_index("tile")
    local_count = landing.shape[1]
    total_rows = landing.shape[2]
    rows_dev = total_rows // n_proj
    cols_dev = chunks * cw
    total_cols = cols_dev * n_tile
    slices, lmax = rw.shape[2], rw.shape[3]
    win_cols = col_w.shape[2]
    vt = col_w.shape[3]
    part_cols = vt // PARTS

    def proj_peer(j):
        return lax.rem(me_p + j, n_proj)

    def proj_source(j):
        return lax.rem(me_p + n_proj - j, n_proj)

    def tile_peer(j):
        return lax.rem(me_t + j, n_tile)

    def tile_source(j):
        return lax.rem(me_t + n_tile - j, n_tile)

    def c_copy(local):
        return pltpu.make_async_copy(
            col_w.at[local, 0], cbuf.at[pl.ds(local * win_cols, win_cols)], c_sem.at[local]
        )

    def own_copy(k):
        return pltpu.make_async_copy(
            raw.at[pl.ds(me_p * local_count, local_count), :, pl.ds(pl.multiple_of(k * cw, cw), cw)],
            landing.at[k, :, pl.ds(pl.multiple_of(me_p * rows_dev, rows_dev), rows_dev)],
            own_sem.at[k],
        )

    def raw_copy(k, j, row_block):
        peer = proj_peer(j)
        return pltpu.make_async_remote_copy(
            src_ref=raw.at[
                pl.ds(peer * local_count, local_count), :, pl.ds(pl.multiple_of(k * cw, cw), cw)
            ],
            dst_ref=landing.at[
                k, :, pl.ds(pl.multiple_of(row_block * rows_dev, rows_dev), rows_dev)
            ],
            send_sem=raw_send.at[k, j],
            recv_sem=raw_recv.at[k, j],
            device_id=(peer, me_t),
            device_id_type=MESH,
        )

    def rw_copy(j, slot):
        return pltpu.make_async_remote_copy(
            src_ref=rw.at[:, 0],
            dst_ref=rwland.at[slot],
            send_sem=rw_send.at[j],
            recv_sem=rw_recv.at[j],
            device_id=(me_p, tile_peer(j)),
            device_id_type=MESH,
        )

    def z_copy(k, j, tile):
        column = pl.multiple_of(128 + tile * cols_dev + k * cw, 128)
        return pltpu.make_async_remote_copy(
            src_ref=ybuf.at[k, tile_peer(j)],
            dst_ref=zbuf.at[:, :, pl.ds(column, cw)],
            send_sem=z_send.at[k, j],
            recv_sem=z_recv.at[k, j],
            device_id=(me_p, tile_peer(j)),
            device_id_type=MESH,
        )

    def p_copy(n, j, slot):
        return pltpu.make_async_remote_copy(
            src_ref=psend.at[n, proj_peer(j)],
            dst_ref=precv.at[n, slot],
            send_sem=p_send.at[n, j],
            recv_sem=p_recv.at[n, j],
            device_id=(proj_peer(j), me_t),
            device_id_type=MESH,
        )

    def each(count, first, f):
        def step(i, carry):
            f(i)
            return carry

        lax.fori_loop(first, count, step, 0)

    barrier = pltpu.get_barrier_semaphore()

    def greet_proj(j):
        pl.semaphore_signal(barrier, inc=1, device_id=(proj_peer(j), me_t), device_id_type=MESH)

    def greet_tile(j):
        pl.semaphore_signal(barrier, inc=1, device_id=(me_p, tile_peer(j)), device_id_type=MESH)

    each(n_proj, 1, greet_proj)
    each(n_tile, 1, greet_tile)
    pl.semaphore_wait(barrier, n_proj + n_tile - 2)

    each(n_tile, 1, lambda j: rw_copy(j, me_t).start())
    for k in range(min(2, chunks)):
        each(n_proj, 1, lambda j: raw_copy(k, j, me_p).start())
    each(chunks, 0, lambda k: own_copy(k).start())
    for local in range(local_count):
        c_copy(local).start()

    edge = jnp.zeros((local_count, slices, 128), zbuf.dtype)
    zbuf[:, :, 0:128] = edge
    zbuf[:, :, 128 + total_cols :] = edge

    rwland[me_t] = rw[:, 0]
    each(n_tile, 1, lambda j: rw_copy(j, tile_source(j)).wait_recv())

    def place(t):
        band_row = lax.broadcasted_iota(jnp.int32, (lmax, total_rows), 0)
        row = lax.broadcasted_iota(jnp.int32, (lmax, total_rows), 1)
        for local in range(local_count):
            start = starts[me_p * local_count + local, t]
            length = lengths[me_p * local_count + local, t]
            hot = (row - band_row == start) & (band_row < length)
            hot = jnp.where(hot, 1.0, 0.0).astype(jnp.bfloat16)
            placed = jnp.dot(rwland[t, local], hot, preferred_element_type=jnp.float32)
            at = pl.ds(pl.multiple_of(t * slices, slices), slices)
            wide[local, at, :] = placed.astype(jnp.bfloat16)

    each(n_tile, 0, place)

    dist = 2.0 * total_cols

    def chunk_step(k):
        each(n_proj, 1, lambda j: raw_copy(k, j, me_p).wait_send())

        @pl.when(k + 2 < chunks)
        def _():
            each(n_proj, 1, lambda j: raw_copy(k + 2, j, me_p).start())

        own_copy(k).wait()
        each(n_proj, 1, lambda j: raw_copy(k, j, proj_source(j)).wait_recv())

        def weigh(b):
            at = pl.ds(pl.multiple_of(b * 128, 128), 128)
            row = b * 128 + lax.broadcasted_iota(jnp.int32, (128, cw), 0)
            column = me_t * cols_dev + k * cw + lax.broadcasted_iota(jnp.int32, (128, cw), 1)
            v = row.astype(jnp.float32) + (0.5 - total_rows / 2.0)
            u = column.astype(jnp.float32) + (0.5 - total_cols / 2.0)
            weight = dist * lax.rsqrt(dist * dist + u * u + v * v)
            for local in range(local_count):
                value = landing[k, local, at, :].astype(jnp.float32) * weight
                weighted[local, at, :] = value.astype(jnp.bfloat16)

        each(total_rows // 128, 0, weigh)

        own_column = pl.multiple_of(128 + me_t * cols_dev + k * cw, 128)

        def mix(t):
            at = pl.ds(pl.multiple_of(t * slices, slices), slices)
            for local in range(local_count):
                y = jnp.dot(
                    wide[local, at, :], weighted[local], preferred_element_type=jnp.float32
                )
                ybuf[k, t, local] = y.astype(jnp.bfloat16)

        each(n_tile, 0, mix)
        each(n_tile, 1, lambda j: z_copy(k, j, me_t).start())
        zbuf[:, :, pl.ds(own_column, cw)] = ybuf[k, me_t]

    each(chunks, 0, chunk_step)

    for local in range(local_count):
        c_copy(local).wait()

    each(n_tile, 1, lambda j: each(chunks, 0, lambda k: z_copy(k, j, tile_source(j)).wait_recv()))

    for local in range(local_count):
        part = zbuf[local]
        bit = 1
        while 2 * bit <= (total_cols - win_cols) // 128:
            bit *= 2
        while bit:
            width = min(win_cols + 256 + 128 * (bit - 1), part.shape[1])
            moved = part[:, 128 * bit : 128 * bit + width]
            if moved.shape[1] < width:
                tail = jnp.zeros((slices, width - moved.shape[1]), part.dtype)
                moved = jnp.concatenate([moved, tail], axis=1)
            skip = jnp.full((slices, width), offsets[local, 0], jnp.int32) & bit
            part = jnp.where(skip != 0, moved, part[:, :width])
            bit //= 2
        for group in range(win_cols // 256):
            value = jnp.dot(
                part[:, 256 * group : 256 * group + 512],
                taps[...],
                preferred_element_type=jnp.float32,
            )
            at = local * win_cols + 256 * group
            filt[:, at : at + 256] = value.astype(jnp.bfloat16)

    for n in range(PARTS):
        for half in range(part_cols // 256):
            at = n * part_cols + 256 * half
            acc = jnp.dot(filt[...], cbuf[:, at : at + 256], preferred_element_type=jnp.float32)
            psend[n, :, :, 256 * half : 256 * half + 256] = acc.reshape(
                n_proj, slices // n_proj, 256
            ).astype(psend.dtype)
        each(n_proj, 1, lambda j: p_copy(n, j, me_p).start())
        precv[n, me_p] = psend[n, me_p]

    for n in range(PARTS):
        each(n_proj, 1, lambda j: p_copy(n, j, proj_source(j)).wait_recv())
        total = precv[n, 0].astype(jnp.float32)
        for source in range(1, n_proj):
            total = total + precv[n, source].astype(jnp.float32)
        out[:, n * part_cols : (n + 1) * part_cols] = total

    each(n_tile, 1, lambda j: rw_copy(j, me_t).wait_send())
    each(n_tile, 1, lambda j: each(chunks, 0, lambda k: z_copy(k, j, me_t).wait_send()))
    for n in range(PARTS):
        each(n_proj, 1, lambda j: p_copy(n, j, me_p).wait_send())


def body(raw, row_weights, col_weights, band_start, band_length, col_offset):
    proj_count, rows_dev, cols_dev = raw.shape
    n_proj = lax.axis_size("proj")
    n_tile = lax.axis_size("tile")
    total_rows = rows_dev * n_proj
    total_cols = cols_dev * n_tile
    local_count, _, slices, lmax = row_weights.shape
    win_cols, vt = col_weights.shape[2:]
    cw = min(CHUNK, cols_dev)
    chunks = cols_dev // cw
    out_rows = slices // n_proj
    sum_type = jnp.bfloat16 if out_rows % 16 == 0 else jnp.float32
    bf16 = jnp.bfloat16
    smem = pl.BlockSpec(memory_space=pltpu.SMEM)
    vmem = pl.BlockSpec(memory_space=pltpu.VMEM)
    hbm = pl.BlockSpec(memory_space=pl.ANY)
    dma = pltpu.SemaphoreType.DMA
    taps = jnp.asarray(tap_matrix())
    flops = 2 * local_count * n_tile * slices * total_rows * cols_dev
    return pl.pallas_call(
        functools.partial(kernel, n_proj, n_tile, chunks, cw),
        out_shape=jax.ShapeDtypeStruct((out_rows, vt), jnp.float32),
        in_specs=[smem, smem, smem, vmem, vmem, hbm, hbm],
        out_specs=vmem,
        scratch_shapes=[
            pltpu.VMEM((chunks, local_count, total_rows, cw), bf16),
            pltpu.VMEM((local_count, n_tile * slices, total_rows), bf16),
            pltpu.VMEM((local_count, total_rows, cw), bf16),
            pltpu.VMEM((chunks, n_tile, local_count, slices, cw), bf16),
            pltpu.VMEM((local_count, slices, total_cols + 256), bf16),
            pltpu.VMEM((n_tile, local_count, slices, lmax), bf16),
            pltpu.VMEM((slices, local_count * win_cols), bf16),
            pltpu.VMEM((local_count * win_cols, vt), bf16),
            pltpu.VMEM((PARTS, n_proj, out_rows, vt // PARTS), sum_type),
            pltpu.VMEM((PARTS, n_proj, out_rows, vt // PARTS), sum_type),
            dma((chunks,)),
            dma((chunks, n_proj)),
            dma((chunks, n_proj)),
            dma((n_tile,)),
            dma((n_tile,)),
            dma((chunks, n_tile)),
            dma((chunks, n_tile)),
            dma((local_count,)),
            dma((PARTS, n_proj)),
            dma((PARTS, n_proj)),
        ],
        compiler_params=pltpu.CompilerParams(
            collective_id=0, has_side_effects=True, vmem_limit_bytes=50 * 1024 * 1024
        ),
        cost_estimate=pl.CostEstimate(
            flops=flops, bytes_accessed=16 * 1024 * 1024, transcendentals=0
        ),
    )(band_start, band_length, col_offset, taps, row_weights, raw, col_weights)


def solution(mesh):
    return jax.shard_map(
        body,
        mesh=mesh,
        in_specs=(
            P(None, "proj", "tile"),
            P("proj", "tile", None, None),
            P("proj", "tile", None, None),
            P(),
            P(),
            P("proj", "tile"),
        ),
        out_specs=P("proj", "tile"),
        check_vma=False,
    )
```

```python
import functools
import math

import jax
import jax.numpy as jnp
import ml_dtypes
import numpy as np
from jax import lax
from jax.experimental import pallas as pl
from jax.experimental.pallas import tpu as pltpu
from jax.sharding import PartitionSpec as P

MESH = pl.DeviceIdType.MESH
CHUNK = 256
PARTS = 4
DEPTH = 3


def tap_matrix():
    n = np.arange(256)[None, :] - np.arange(512)[:, None] + 128
    n_f = np.where(n == 0, 1, n).astype(np.float32)
    odd = -np.float32(1.0) / (np.float32(math.pi * math.pi) * (n_f * n_f))
    value = np.where(n == 0, np.float32(0.25), np.where(n % 2 != 0, odd, np.float32(0.0)))
    value = np.where((n >= -128) & (n <= 127), value, np.float32(0.0))
    return value.astype(ml_dtypes.bfloat16)


def kernel(
    n_proj, n_tile, chunks, cw,
    starts_in, lengths_in, offsets_in, taps_in, rw, raw, col_w, out,
    starts, lengths, offsets, taps,
    landing, wide, weighted, ybuf, zbuf, rwland, filt, cbuf, acc, psend, precv,
    int_sem, tap_sem, own_sem, raw_send, raw_recv, rw_own, rw_send, rw_recv, z_send, z_recv,
    c_sem, p_send, p_recv,
):
    me_p = lax.axis_index("proj")
    me_t = lax.axis_index("tile")
    local_count = landing.shape[1]
    total_rows = landing.shape[2]
    rows_dev = total_rows // n_proj
    cols_dev = chunks * cw
    total_cols = cols_dev * n_tile
    slices, lmax = rw.shape[2], rw.shape[3]
    win_cols = col_w.shape[2]
    vt = col_w.shape[3]
    part_cols = vt // PARTS
    steps = local_count * chunks

    def proj_peer(j):
        return lax.rem(me_p + j, n_proj)

    def proj_source(j):
        return lax.rem(me_p + n_proj - j, n_proj)

    def tile_peer(j):
        return lax.rem(me_t + j, n_tile)

    def tile_source(j):
        return lax.rem(me_t + n_tile - j, n_tile)

    def c_copy(local):
        return pltpu.make_async_copy(col_w.at[local, 0], cbuf.at[local], c_sem.at[local])

    def raw_place(s, row_block):
        rows = pl.ds(pl.multiple_of(row_block * rows_dev, rows_dev), rows_dev)
        return landing.at[lax.rem(s, chunks), lax.div(s, chunks), rows]

    def raw_piece(s, peer):
        columns = pl.ds(pl.multiple_of(lax.rem(s, chunks) * cw, cw), cw)
        return raw.at[peer * local_count + lax.div(s, chunks), :, columns]

    def own_copy(s):
        return pltpu.make_async_copy(raw_piece(s, me_p), raw_place(s, me_p), own_sem.at[s])

    def raw_copy(s, j, row_block):
        peer = proj_peer(j)
        return pltpu.make_async_remote_copy(
            src_ref=raw_piece(s, peer),
            dst_ref=raw_place(s, row_block),
            send_sem=raw_send.at[s, j],
            recv_sem=raw_recv.at[s, j],
            device_id=(peer, me_t),
            device_id_type=MESH,
        )

    def rw_copy(j, slot):
        return pltpu.make_async_remote_copy(
            src_ref=rw.at[:, 0],
            dst_ref=rwland.at[slot],
            send_sem=rw_send.at[j],
            recv_sem=rw_recv.at[j],
            device_id=(me_p, tile_peer(j)),
            device_id_type=MESH,
        )

    def z_place(s, tile):
        column = pl.multiple_of(128 + tile * cols_dev + lax.rem(s, chunks) * cw, 128)
        return zbuf.at[lax.div(s, chunks), :, pl.ds(column, cw)]

    def z_copy(s, j, tile):
        return pltpu.make_async_remote_copy(
            src_ref=ybuf.at[s, tile_peer(j)],
            dst_ref=z_place(s, tile),
            send_sem=z_send.at[s, j],
            recv_sem=z_recv.at[s, j],
            device_id=(me_p, tile_peer(j)),
            device_id_type=MESH,
        )

    def p_copy(n, j, slot):
        return pltpu.make_async_remote_copy(
            src_ref=psend.at[n, proj_peer(j)],
            dst_ref=precv.at[n, slot],
            send_sem=p_send.at[n, j],
            recv_sem=p_recv.at[n, j],
            device_id=(proj_peer(j), me_t),
            device_id_type=MESH,
        )

    def each(count, first, f):
        def step(i, carry):
            f(i)
            return carry

        lax.fori_loop(first, count, step, 0)

    barrier = pltpu.get_barrier_semaphore()

    def greet_proj(j):
        pl.semaphore_signal(barrier, inc=1, device_id=(proj_peer(j), me_t), device_id_type=MESH)

    def greet_tile(j):
        pl.semaphore_signal(barrier, inc=1, device_id=(me_p, tile_peer(j)), device_id_type=MESH)

    each(n_proj, 1, greet_proj)
    each(n_tile, 1, greet_tile)

    small = [
        pltpu.make_async_copy(starts_in, starts, int_sem.at[0]),
        pltpu.make_async_copy(lengths_in, lengths, int_sem.at[1]),
        pltpu.make_async_copy(offsets_in, offsets, int_sem.at[2]),
        pltpu.make_async_copy(rw.at[:, 0], rwland.at[me_t], rw_own),
        pltpu.make_async_copy(taps_in, taps, tap_sem),
    ]
    for copy in small:
        copy.start()
    each(steps, 0, lambda s: own_copy(s).start())
    edge = jnp.zeros((local_count, slices, 128), zbuf.dtype)
    zbuf[:, :, 0:128] = edge
    zbuf[:, :, 128 + total_cols :] = edge

    pl.semaphore_wait(barrier, n_proj + n_tile - 2)

    each(n_tile, 1, lambda j: rw_copy(j, me_t).start())
    for s in range(min(DEPTH, steps)):
        each(n_proj, 1, lambda j: raw_copy(s, j, me_p).start())
    for local in range(local_count):
        c_copy(local).start()
    for copy in small:
        copy.wait()
    each(n_tile, 1, lambda j: rw_copy(j, tile_source(j)).wait_recv())

    def place(local, t):
        band_row = lax.broadcasted_iota(jnp.int32, (lmax, total_rows), 0)
        row = lax.broadcasted_iota(jnp.int32, (lmax, total_rows), 1)
        at = pl.ds(me_p * local_count + local, 1)
        start = starts[at, t : t + 1]
        length = lengths[at, t : t + 1]
        hot = (row - band_row == start) & (band_row < length)
        hot = jnp.where(hot, 1.0, 0.0).astype(jnp.bfloat16)
        placed = jnp.dot(rwland[t, local], hot, preferred_element_type=jnp.float32)
        wide[local, t * slices : (t + 1) * slices, :] = placed.astype(jnp.bfloat16)

    dist = 2.0 * total_cols

    def step(s):
        c, local = lax.rem(s, chunks), lax.div(s, chunks)
        each(n_proj, 1, lambda j: raw_copy(s, j, me_p).wait_send())

        @pl.when(s + DEPTH < steps)
        def _():
            each(n_proj, 1, lambda j: raw_copy(s + DEPTH, j, me_p).start())

        own_copy(s).wait()
        each(n_proj, 1, lambda j: raw_copy(s, j, proj_source(j)).wait_recv())

        def weigh(b):
            at = pl.ds(pl.multiple_of(b * 128, 128), 128)
            row = b * 128 + lax.broadcasted_iota(jnp.int32, (128, cw), 0)
            column = me_t * cols_dev + c * cw + lax.broadcasted_iota(jnp.int32, (128, cw), 1)
            v = row.astype(jnp.float32) + (0.5 - total_rows / 2.0)
            u = column.astype(jnp.float32) + (0.5 - total_cols / 2.0)
            weight = dist * lax.rsqrt(dist * dist + u * u + v * v)
            value = landing[c, local, at, :].astype(jnp.float32) * weight
            weighted[at, :] = value.astype(jnp.bfloat16)

        each(total_rows // 128, 0, weigh)

        def mix(t):
            at = pl.ds(pl.multiple_of(t * slices, slices), slices)
            y = jnp.dot(wide[local, at, :], weighted[...], preferred_element_type=jnp.float32)
            ybuf[s, t] = y.astype(jnp.bfloat16)

        each(n_tile, 0, mix)
        each(n_tile, 1, lambda j: z_copy(s, j, me_t).start())
        column = pl.multiple_of(128 + me_t * cols_dev + c * cw, 128)
        zbuf[local, :, pl.ds(column, cw)] = ybuf[s, me_t]

    def window(local):
        def arrived(s):
            each(n_tile, 1, lambda j: z_copy(s, j, tile_source(j)).wait_recv())

        each((local + 1) * chunks, local * chunks, arrived)
        part = zbuf[local]
        offset = offsets[local : local + 1, :]
        bit = 1
        while 2 * bit <= (total_cols - win_cols) // 128:
            bit *= 2
        while bit:
            width = min(win_cols + 256 + 128 * (bit - 1), part.shape[1])
            moved = part[:, 128 * bit : 128 * bit + width]
            if moved.shape[1] < width:
                tail = jnp.zeros((slices, width - moved.shape[1]), part.dtype)
                moved = jnp.concatenate([moved, tail], axis=1)
            skip = jnp.broadcast_to(offset, (slices, width)) & bit
            part = jnp.where(skip != 0, moved, part[:, :width])
            bit //= 2
        for group in range(win_cols // 256):
            value = jnp.dot(
                part[:, 256 * group : 256 * group + 512],
                taps[...],
                preferred_element_type=jnp.float32,
            )
            filt[local, :, 256 * group : 256 * group + 256] = value.astype(jnp.bfloat16)

    def product(local, at):
        return jnp.dot(
            filt[local], cbuf[local, :, at : at + 256], preferred_element_type=jnp.float32
        )

    def add_up(local):
        window(local)
        c_copy(local).wait()
        for at in range(0, vt, 256):
            value = product(local, at)
            acc[:, at : at + 256] = value if local == 0 else acc[:, at : at + 256] + value

    done = 0
    for local in range(local_count):
        for t in range(n_tile):
            place(local, t)
        if local > 0:
            until = min(local * chunks + 2, steps)
            each(until, done, step)
            done = until
            add_up(local - 1)
        else:
            done = min(chunks - 1, 2)
            each(done, 0, step)
    each(steps, done, step)

    last = local_count - 1
    window(last)
    c_copy(last).wait()
    for n in range(PARTS):
        for half in range(part_cols // 256):
            at = n * part_cols + 256 * half
            value = product(last, at)
            if last > 0:
                value = value + acc[:, at : at + 256]
            psend[n, :, :, 256 * half : 256 * half + 256] = value.reshape(
                n_proj, slices // n_proj, 256
            ).astype(psend.dtype)
        each(n_proj, 1, lambda j: p_copy(n, j, me_p).start())
        precv[n, me_p] = psend[n, me_p]

    for n in range(PARTS):
        each(n_proj, 1, lambda j: p_copy(n, j, proj_source(j)).wait_recv())
        total = precv[n, 0].astype(jnp.float32)
        for source in range(1, n_proj):
            total = total + precv[n, source].astype(jnp.float32)
        out[:, n * part_cols : (n + 1) * part_cols] = total

    each(n_tile, 1, lambda j: rw_copy(j, me_t).wait_send())
    each(n_tile, 1, lambda j: each(steps, 0, lambda s: z_copy(s, j, me_t).wait_send()))
    for n in range(PARTS):
        each(n_proj, 1, lambda j: p_copy(n, j, me_p).wait_send())


def body(raw, row_weights, col_weights, band_start, band_length, col_offset):
    proj_count, rows_dev, cols_dev = raw.shape
    n_proj = lax.axis_size("proj")
    n_tile = lax.axis_size("tile")
    total_rows = rows_dev * n_proj
    total_cols = cols_dev * n_tile
    local_count, _, slices, lmax = row_weights.shape
    win_cols, vt = col_weights.shape[2:]
    cw = min(CHUNK, cols_dev)
    chunks = cols_dev // cw
    steps = local_count * chunks
    out_rows = slices // n_proj
    sum_type = jnp.bfloat16 if out_rows % 16 == 0 else jnp.float32
    bf16 = jnp.bfloat16
    vmem = pl.BlockSpec(memory_space=pltpu.VMEM)
    hbm = pl.BlockSpec(memory_space=pl.ANY)
    dma = pltpu.SemaphoreType.DMA
    taps = jnp.asarray(tap_matrix())
    flops = 2 * local_count * n_tile * slices * total_rows * cols_dev
    return pl.pallas_call(
        functools.partial(kernel, n_proj, n_tile, chunks, cw),
        out_shape=jax.ShapeDtypeStruct((out_rows, vt), jnp.float32),
        in_specs=[hbm] * 7,
        out_specs=vmem,
        scratch_shapes=[
            pltpu.VMEM(band_start.shape, jnp.int32),
            pltpu.VMEM(band_length.shape, jnp.int32),
            pltpu.VMEM(col_offset.shape, jnp.int32),
            pltpu.VMEM(taps.shape, bf16),
            pltpu.VMEM((chunks, local_count, total_rows, cw), bf16),
            pltpu.VMEM((local_count, n_tile * slices, total_rows), bf16),
            pltpu.VMEM((total_rows, cw), bf16),
            pltpu.VMEM((steps, n_tile, slices, cw), bf16),
            pltpu.VMEM((local_count, slices, total_cols + 256), bf16),
            pltpu.VMEM((n_tile, local_count, slices, lmax), bf16),
            pltpu.VMEM((local_count, slices, win_cols), bf16),
            pltpu.VMEM((local_count, win_cols, vt), bf16),
            pltpu.VMEM((slices, vt), jnp.float32),
            pltpu.VMEM((PARTS, n_proj, out_rows, vt // PARTS), sum_type),
            pltpu.VMEM((PARTS, n_proj, out_rows, vt // PARTS), sum_type),
            dma((3,)),
            dma,
            dma((steps,)),
            dma((steps, n_proj)),
            dma((steps, n_proj)),
            dma,
            dma((n_tile,)),
            dma((n_tile,)),
            dma((steps, n_tile)),
            dma((steps, n_tile)),
            dma((local_count,)),
            dma((PARTS, n_proj)),
            dma((PARTS, n_proj)),
        ],
        compiler_params=pltpu.CompilerParams(
            collective_id=0, has_side_effects=True, vmem_limit_bytes=50 * 1024 * 1024
        ),
        cost_estimate=pl.CostEstimate(
            flops=flops, bytes_accessed=16 * 1024 * 1024, transcendentals=0
        ),
    )(band_start, band_length, col_offset, taps, row_weights, raw, col_weights)


def solution(mesh):
    return jax.shard_map(
        body,
        mesh=mesh,
        in_specs=(
            P(None, "proj", "tile"),
            P("proj", "tile", None, None),
            P("proj", "tile", None, None),
            P(),
            P(),
            P("proj", "tile"),
        ),
        out_specs=P("proj", "tile"),
        check_vma=False,
    )
```

```python
import functools
import math

import jax
import jax.numpy as jnp
from jax import lax
from jax.experimental import pallas as pl
from jax.experimental.pallas import tpu as pltpu
from jax.sharding import PartitionSpec as P

MESH = pl.DeviceIdType.MESH
CHUNK = 128
PARTS = 4
DEPTH = 6
VMEM_BYTES = 63 * 1024 * 1024


def tap_matrix():
    row = lax.broadcasted_iota(jnp.int32, (512, 256), 0)
    n = lax.broadcasted_iota(jnp.int32, (512, 256), 1) - row + 128
    n_f = n.astype(jnp.float32)
    safe_sq = jnp.where(n == 0, 1.0, n_f * n_f)
    odd = jnp.where((n & 1) != 0, -1.0 / (math.pi * math.pi * safe_sq), 0.0)
    value = jnp.where(n == 0, 0.25, odd)
    value = jnp.where((n >= -128) & (n <= 127), value, 0.0)
    return value.astype(jnp.bfloat16)


def kernel(
    n_proj, n_tile, chunks, cw,
    starts_in, lengths_in, offsets_in, rw, raw, col_w, out,
    starts, lengths, offsets, taps,
    landing, wide, weighted, ybuf, zbuf, rwland, filt, cbuf, acc, psend, precv,
    int_sem, own_sem, raw_send, raw_recv, rw_own, rw_send, rw_recv, z_send, z_recv,
    c_sem, p_send, p_recv,
):
    me_p = lax.axis_index("proj")
    me_t = lax.axis_index("tile")
    local_count = landing.shape[1]
    total_rows = landing.shape[2]
    rows_dev = total_rows // n_proj
    cols_dev = chunks * cw
    total_cols = cols_dev * n_tile
    slices, lmax = rw.shape[2], rw.shape[3]
    win_cols = col_w.shape[2]
    vt = col_w.shape[3]
    part_cols = vt // PARTS
    steps = local_count * chunks

    def proj_peer(j):
        mask = mask_of(j)
        peer, bit = me_p, 1
        while bit < n_proj:
            change = lax.rem(lax.div(mask, bit), 2)
            mine = lax.rem(lax.div(me_p, bit), 2)
            peer = peer + bit * change * (1 - 2 * mine)
            bit *= 2
        return peer

    def mask_of(j):
        mask = lax.rem(2 * j, n_proj) + lax.div(2 * j, n_proj)
        one, two = lax.rem(lax.div(mask, 2), 2), lax.rem(lax.div(mask, 4), 2)
        return mask + 2 * (two - one) * lax.rem(me_p, 2) - 4 * (two - one) * lax.rem(me_p, 2)

    def tile_peer(j):
        return lax.rem(me_t + j, n_tile)

    def tile_source(j):
        return lax.rem(me_t + n_tile - j, n_tile)

    def c_copy(local):
        return pltpu.make_async_copy(col_w.at[local, 0], cbuf.at[local], c_sem.at[local])

    def raw_place(s, row_block):
        rows = pl.ds(pl.multiple_of(row_block * rows_dev, rows_dev), rows_dev)
        return landing.at[lax.rem(s, chunks), lax.div(s, chunks), rows]

    def raw_piece(s, peer):
        columns = pl.ds(pl.multiple_of(lax.rem(s, chunks) * cw, cw), cw)
        return raw.at[peer * local_count + lax.div(s, chunks), :, columns]

    def own_copy(s):
        return pltpu.make_async_copy(raw_piece(s, me_p), raw_place(s, me_p), own_sem.at[s])

    def raw_copy(s, j, row_block):
        peer = proj_peer(j)
        return pltpu.make_async_remote_copy(
            src_ref=raw_piece(s, peer),
            dst_ref=raw_place(s, row_block),
            send_sem=raw_send.at[s, mask_of(j)],
            recv_sem=raw_recv.at[s, mask_of(j)],
            device_id=(peer, me_t),
            device_id_type=MESH,
        )

    def rw_copy(j, slot):
        return pltpu.make_async_remote_copy(
            src_ref=rw.at[:, 0],
            dst_ref=rwland.at[slot],
            send_sem=rw_send.at[j],
            recv_sem=rw_recv.at[j],
            device_id=(me_p, tile_peer(j)),
            device_id_type=MESH,
        )

    def z_place(s, tile):
        column = pl.multiple_of(128 + tile * cols_dev + lax.rem(s, chunks) * cw, 128)
        return zbuf.at[lax.div(s, chunks), :, pl.ds(column, cw)]

    def z_copy(s, j, tile):
        return pltpu.make_async_remote_copy(
            src_ref=ybuf.at[s, tile_peer(j)],
            dst_ref=z_place(s, tile),
            send_sem=z_send.at[s, j],
            recv_sem=z_recv.at[s, j],
            device_id=(me_p, tile_peer(j)),
            device_id_type=MESH,
        )

    def p_copy(n, j, slot):
        return pltpu.make_async_remote_copy(
            src_ref=psend.at[n, proj_peer(j)],
            dst_ref=precv.at[n, slot],
            send_sem=p_send.at[n, mask_of(j)],
            recv_sem=p_recv.at[n, mask_of(j)],
            device_id=(proj_peer(j), me_t),
            device_id_type=MESH,
        )

    def each(count, first, f):
        def step(i, carry):
            f(i)
            return carry

        lax.fori_loop(first, count, step, 0)

    barrier = pltpu.get_barrier_semaphore()

    def greet_proj(j):
        pl.semaphore_signal(barrier, inc=1, device_id=(proj_peer(j), me_t), device_id_type=MESH)

    def greet_tile(j):
        pl.semaphore_signal(barrier, inc=1, device_id=(me_p, tile_peer(j)), device_id_type=MESH)

    each(n_proj, 1, greet_proj)
    each(n_tile, 1, greet_tile)

    small = [
        pltpu.make_async_copy(starts_in, starts, int_sem.at[0]),
        pltpu.make_async_copy(lengths_in, lengths, int_sem.at[1]),
        pltpu.make_async_copy(offsets_in, offsets, int_sem.at[2]),
        pltpu.make_async_copy(rw.at[:, 0], rwland.at[me_t], rw_own),
    ]
    for copy in small:
        copy.start()
    each(steps, 0, lambda s: own_copy(s).start())
    edge = jnp.zeros((local_count, slices, 128), zbuf.dtype)
    zbuf[:, :, 0:128] = edge
    zbuf[:, :, 128 + total_cols :] = edge

    pl.semaphore_wait(barrier, n_proj + n_tile - 2)

    each(n_tile, 1, lambda j: rw_copy(j, me_t).start())
    for s in range(min(DEPTH, steps)):
        each(n_proj, 1, lambda j: raw_copy(s, j, me_p).start())
    for local in range(local_count):
        c_copy(local).start()
    taps[...] = tap_matrix()
    for copy in small:
        copy.wait()
    each(n_tile, 1, lambda j: rw_copy(j, tile_source(j)).wait_recv())

    def place(local, t):
        band_row = lax.broadcasted_iota(jnp.int32, (lmax, total_rows), 0)
        row = lax.broadcasted_iota(jnp.int32, (lmax, total_rows), 1)
        mine = lax.broadcasted_iota(jnp.int32, (1, starts.shape[1]), 1)
        mine = mine == me_p * local_count + local
        start = jnp.sum(jnp.where(mine, starts[t : t + 1, :], 0), axis=1, keepdims=True)
        length = jnp.sum(jnp.where(mine, lengths[t : t + 1, :], 0), axis=1, keepdims=True)
        hot = (row - band_row == start) & (band_row < length)
        hot = jnp.where(hot, 1.0, 0.0).astype(jnp.bfloat16)
        placed = jnp.dot(rwland[t, local], hot, preferred_element_type=jnp.float32)
        wide[local, t * slices : (t + 1) * slices, :] = placed.astype(jnp.bfloat16)

    dist = 2.0 * total_cols

    def step(s):
        c, local = lax.rem(s, chunks), lax.div(s, chunks)
        each(n_proj, 1, lambda j: raw_copy(s, j, me_p).wait_send())

        @pl.when(s + DEPTH < steps)
        def _():
            each(n_proj, 1, lambda j: raw_copy(s + DEPTH, j, me_p).start())

        own_copy(s).wait()
        each(n_proj, 1, lambda j: raw_copy(s, j, proj_peer(j)).wait_recv())

        def weigh(b):
            at = pl.ds(pl.multiple_of(b * 128, 128), 128)
            row = b * 128 + lax.broadcasted_iota(jnp.int32, (128, cw), 0)
            column = me_t * cols_dev + c * cw + lax.broadcasted_iota(jnp.int32, (128, cw), 1)
            v = row.astype(jnp.float32) + (0.5 - total_rows / 2.0)
            u = column.astype(jnp.float32) + (0.5 - total_cols / 2.0)
            weight = dist * lax.rsqrt(dist * dist + u * u + v * v)
            value = landing[c, local, at, :].astype(jnp.float32) * weight
            weighted[at, :] = value.astype(jnp.bfloat16)

        each(total_rows // 128, 0, weigh)

        y = jnp.dot(wide[local], weighted[...], preferred_element_type=jnp.float32)
        ybuf[s] = y.astype(jnp.bfloat16).reshape(n_tile, slices, cw)
        each(n_tile, 1, lambda j: z_copy(s, j, me_t).start())
        column = pl.multiple_of(128 + me_t * cols_dev + c * cw, 128)
        zbuf[local, :, pl.ds(column, cw)] = ybuf[s, me_t]

    def window(local):
        def arrived(s):
            each(n_tile, 1, lambda j: z_copy(s, j, tile_source(j)).wait_recv())

        each((local + 1) * chunks, local * chunks, arrived)
        part = zbuf[local]
        offset = offsets[:, local : local + 1]
        bit = 1
        while 2 * bit <= (total_cols - win_cols) // 128:
            bit *= 2
        while bit:
            width = min(win_cols + 256 + 128 * (bit - 1), part.shape[1])
            moved = part[:, 128 * bit : 128 * bit + width]
            if moved.shape[1] < width:
                tail = jnp.zeros((slices, width - moved.shape[1]), part.dtype)
                moved = jnp.concatenate([moved, tail], axis=1)
            skip = jnp.broadcast_to(offset, (slices, width)) & bit
            part = jnp.where(skip != 0, moved, part[:, :width])
            bit //= 2
        for group in range(win_cols // 256):
            value = jnp.dot(
                part[:, 256 * group : 256 * group + 512],
                taps[...],
                preferred_element_type=jnp.float32,
            )
            filt[local, :, 256 * group : 256 * group + 256] = value.astype(jnp.bfloat16)

    def product(local, at):
        return jnp.dot(
            filt[local], cbuf[local, :, at : at + 256], preferred_element_type=jnp.float32
        )

    def add_up(local):
        window(local)
        c_copy(local).wait()
        for at in range(0, vt, 256):
            value = product(local, at)
            acc[:, at : at + 256] = value if local == 0 else acc[:, at : at + 256] + value

    done = 0
    for local in range(local_count):
        for t in range(n_tile):
            place(local, t)
        if local > 0:
            until = min(local * chunks + 2, steps)
            each(until, done, step)
            done = until
            add_up(local - 1)
        else:
            done = min(chunks - 1, 2)
            each(done, 0, step)
    each(steps, done, step)

    last = local_count - 1
    window(last)
    c_copy(last).wait()
    for n in range(PARTS):
        for half in range(part_cols // 256):
            at = n * part_cols + 256 * half
            value = product(last, at)
            if last > 0:
                value = value + acc[:, at : at + 256]
            psend[n, :, :, 256 * half : 256 * half + 256] = value.reshape(
                n_proj, slices // n_proj, 256
            ).astype(psend.dtype)
        each(n_proj, 1, lambda j: p_copy(n, j, me_p).start())
        precv[n, me_p] = psend[n, me_p]

    for n in range(PARTS):
        each(n_proj, 1, lambda j: p_copy(n, j, proj_peer(j)).wait_recv())
        total = precv[n, 0].astype(jnp.float32)
        for source in range(1, n_proj):
            total = total + precv[n, source].astype(jnp.float32)
        out[:, n * part_cols : (n + 1) * part_cols] = total

    each(n_tile, 1, lambda j: rw_copy(j, me_t).wait_send())
    each(n_tile, 1, lambda j: each(steps, 0, lambda s: z_copy(s, j, me_t).wait_send()))
    for n in range(PARTS):
        each(n_proj, 1, lambda j: p_copy(n, j, me_p).wait_send())


def body(raw, row_weights, col_weights, band_start, band_length, col_offset):
    proj_count, rows_dev, cols_dev = raw.shape
    n_proj = lax.axis_size("proj")
    n_tile = lax.axis_size("tile")
    total_rows = rows_dev * n_proj
    total_cols = cols_dev * n_tile
    local_count, _, slices, lmax = row_weights.shape
    win_cols, vt = col_weights.shape[2:]
    cw = min(CHUNK, cols_dev)
    chunks = cols_dev // cw
    steps = local_count * chunks
    out_rows = slices // n_proj
    sum_type = jnp.bfloat16 if out_rows % 16 == 0 else jnp.float32
    bf16 = jnp.bfloat16
    vmem = pl.BlockSpec(memory_space=pltpu.VMEM)
    hbm = pl.BlockSpec(memory_space=pl.ANY)
    dma = pltpu.SemaphoreType.DMA
    flops = 2 * local_count * n_tile * slices * total_rows * cols_dev
    return pl.pallas_call(
        functools.partial(kernel, n_proj, n_tile, chunks, cw),
        out_shape=jax.ShapeDtypeStruct((out_rows, vt), jnp.float32),
        in_specs=[hbm] * 6,
        out_specs=vmem,
        scratch_shapes=[
            pltpu.VMEM((n_tile, proj_count), jnp.int32),
            pltpu.VMEM((n_tile, proj_count), jnp.int32),
            pltpu.VMEM((1, local_count), jnp.int32),
            pltpu.VMEM((512, 256), bf16),
            pltpu.VMEM((chunks, local_count, total_rows, cw), bf16),
            pltpu.VMEM((local_count, n_tile * slices, total_rows), bf16),
            pltpu.VMEM((total_rows, cw), bf16),
            pltpu.VMEM((steps, n_tile, slices, cw), bf16),
            pltpu.VMEM((local_count, slices, total_cols + 256), bf16),
            pltpu.VMEM((n_tile, local_count, slices, lmax), bf16),
            pltpu.VMEM((local_count, slices, win_cols), bf16),
            pltpu.VMEM((local_count, win_cols, vt), bf16),
            pltpu.VMEM((slices, vt), jnp.float32),
            pltpu.VMEM((PARTS, n_proj, out_rows, vt // PARTS), sum_type),
            pltpu.VMEM((PARTS, n_proj, out_rows, vt // PARTS), sum_type),
            dma((3,)),
            dma((steps,)),
            dma((steps, n_proj)),
            dma((steps, n_proj)),
            dma,
            dma((n_tile,)),
            dma((n_tile,)),
            dma((steps, n_tile)),
            dma((steps, n_tile)),
            dma((local_count,)),
            dma((PARTS, n_proj)),
            dma((PARTS, n_proj)),
        ],
        compiler_params=pltpu.CompilerParams(
            collective_id=0, has_side_effects=True, vmem_limit_bytes=VMEM_BYTES
        ),
        cost_estimate=pl.CostEstimate(
            flops=flops, bytes_accessed=16 * 1024 * 1024, transcendentals=0
        ),
    )(band_start.T, band_length.T, col_offset.T, row_weights, raw, col_weights)


def solution(mesh):
    return jax.shard_map(
        body,
        mesh=mesh,
        in_specs=(
            P(None, "proj", "tile"),
            P("proj", "tile", None, None),
            P("proj", "tile", None, None),
            P(),
            P(),
            P("proj", "tile"),
        ),
        out_specs=P("proj", "tile"),
        check_vma=False,
    )
```

```python
import functools
import math

import jax
import jax.numpy as jnp
from jax import lax
from jax.experimental import pallas as pl
from jax.experimental.pallas import tpu as pltpu
from jax.sharding import PartitionSpec as P

MESH = pl.DeviceIdType.MESH
CHUNK = 256
PARTS = 4
DEPTH = 3
VMEM_BYTES = 63 * 1024 * 1024


def tap_matrix():
    row = lax.broadcasted_iota(jnp.int32, (512, 256), 0)
    n = lax.broadcasted_iota(jnp.int32, (512, 256), 1) - row + 128
    n_f = n.astype(jnp.float32)
    safe_sq = jnp.where(n == 0, 1.0, n_f * n_f)
    odd = jnp.where((n & 1) != 0, -1.0 / (math.pi * math.pi * safe_sq), 0.0)
    value = jnp.where(n == 0, 0.25, odd)
    value = jnp.where((n >= -128) & (n <= 127), value, 0.0)
    return value.astype(jnp.bfloat16)


def kernel(
    n_proj, n_tile, chunks, cw,
    starts_in, lengths_in, offsets_in, rw, raw, col_w, out,
    starts, lengths, offsets, taps,
    landing, wide, weighted, ybuf, zbuf, rwland, filt, cbuf, acc, psend, precv,
    int_sem, own_sem, raw_send, raw_recv, rw_own, rw_send, rw_recv, z_send, z_recv,
    c_sem, p_send, p_recv,
):
    me_p = lax.axis_index("proj")
    me_t = lax.axis_index("tile")
    local_count = landing.shape[1]
    total_rows = landing.shape[2]
    rows_dev = total_rows // n_proj
    cols_dev = chunks * cw
    total_cols = cols_dev * n_tile
    slices, lmax = rw.shape[2], rw.shape[3]
    win_cols = col_w.shape[2]
    vt = col_w.shape[3]
    part_cols = vt // PARTS
    steps = local_count * chunks

    core = lax.rem(me_p, 2)
    bits, bit = [], 1
    while bit < n_proj:
        bits.append(bit * (1 - 2 * lax.rem(lax.div(me_p, bit), 2)))
        bit *= 2

    def flipped(mask):
        return sum(((mask >> i) & 1) * step for i, step in enumerate(bits))

    proj_peers = {}
    for j in [*range(2, n_proj, 2), *range(n_proj - 1, 0, -2)]:
        other = (j & ~6) | ((j & 2) << 1) | ((j & 4) >> 1) if j % 2 == 0 and n_proj > 4 else j
        proj_peers[j] = me_p + flipped(j) + core * (flipped(other) - flipped(j))
    tile_peers = {j: lax.rem(me_t + j, n_tile) for j in range(1, n_tile)}
    tile_sources = {j: lax.rem(me_t + n_tile - j, n_tile) for j in range(1, n_tile)}

    def proj_peer(j):
        return proj_peers[j]

    def tile_peer(j):
        return tile_peers[j]

    def tile_source(j):
        return tile_sources[j]

    def c_copy(local):
        return pltpu.make_async_copy(col_w.at[local, 0], cbuf.at[local], c_sem.at[local])

    def raw_place(s, row_block):
        rows = pl.ds(pl.multiple_of(row_block * rows_dev, rows_dev), rows_dev)
        return landing.at[lax.rem(s, chunks), lax.div(s, chunks), rows]

    def raw_piece(s, peer):
        columns = pl.ds(pl.multiple_of(lax.rem(s, chunks) * cw, cw), cw)
        return raw.at[peer * local_count + lax.div(s, chunks), :, columns]

    def own_copy(s):
        return pltpu.make_async_copy(raw_piece(s, me_p), raw_place(s, me_p), own_sem.at[s])

    def raw_copy(s, j, row_block):
        peer = proj_peer(j)
        return pltpu.make_async_remote_copy(
            src_ref=raw_piece(s, peer),
            dst_ref=raw_place(s, row_block),
            send_sem=raw_send.at[s, j],
            recv_sem=raw_recv.at[s, j],
            device_id=(peer, me_t),
            device_id_type=MESH,
        )

    def rw_copy(j, slot):
        return pltpu.make_async_remote_copy(
            src_ref=rw.at[:, 0],
            dst_ref=rwland.at[slot],
            send_sem=rw_send.at[j],
            recv_sem=rw_recv.at[j],
            device_id=(me_p, tile_peer(j)),
            device_id_type=MESH,
        )

    def z_place(s, tile):
        column = pl.multiple_of(128 + tile * cols_dev + lax.rem(s, chunks) * cw, 128)
        return zbuf.at[lax.div(s, chunks), :, pl.ds(column, cw)]

    def z_copy(s, j, tile):
        return pltpu.make_async_remote_copy(
            src_ref=ybuf.at[s, tile_peer(j)],
            dst_ref=z_place(s, tile),
            send_sem=z_send.at[s, j],
            recv_sem=z_recv.at[s, j],
            device_id=(me_p, tile_peer(j)),
            device_id_type=MESH,
        )

    def p_copy(n, j, slot):
        return pltpu.make_async_remote_copy(
            src_ref=psend.at[n, proj_peer(j)],
            dst_ref=precv.at[n, slot],
            send_sem=p_send.at[n, j],
            recv_sem=p_recv.at[n, j],
            device_id=(proj_peer(j), me_t),
            device_id_type=MESH,
        )

    def each(count, first, f):
        def step(i, carry):
            f(i)
            return carry

        lax.fori_loop(first, count, step, 0)

    def each_proj(f):
        for j in proj_peers:
            f(j)

    def each_tile(f):
        for j in tile_peers:
            f(j)

    barrier = pltpu.get_barrier_semaphore()

    def greet_proj(j):
        pl.semaphore_signal(barrier, inc=1, device_id=(proj_peer(j), me_t), device_id_type=MESH)

    def greet_tile(j):
        pl.semaphore_signal(barrier, inc=1, device_id=(me_p, tile_peer(j)), device_id_type=MESH)

    each_proj(greet_proj)
    each_tile(greet_tile)

    small = [
        pltpu.make_async_copy(starts_in, starts, int_sem.at[0]),
        pltpu.make_async_copy(lengths_in, lengths, int_sem.at[1]),
        pltpu.make_async_copy(offsets_in, offsets, int_sem.at[2]),
        pltpu.make_async_copy(rw.at[:, 0], rwland.at[me_t], rw_own),
    ]
    for copy in small:
        copy.start()
    each(steps, 0, lambda s: own_copy(s).start())
    edge = jnp.zeros((local_count, slices, 128), zbuf.dtype)
    zbuf[:, :, 0:128] = edge
    zbuf[:, :, 128 + total_cols :] = edge

    pl.semaphore_wait(barrier, n_proj + n_tile - 2)

    each_tile(lambda j: rw_copy(j, me_t).start())
    for s in range(min(DEPTH, steps)):
        each_proj(lambda j: raw_copy(s, j, me_p).start())
    for local in range(local_count):
        c_copy(local).start()
    taps[...] = tap_matrix()
    for copy in small:
        copy.wait()
    each_tile(lambda j: rw_copy(j, tile_source(j)).wait_recv())

    def place(local, t):
        band_row = lax.broadcasted_iota(jnp.int32, (lmax, total_rows), 0)
        row = lax.broadcasted_iota(jnp.int32, (lmax, total_rows), 1)
        mine = lax.broadcasted_iota(jnp.int32, (1, starts.shape[1]), 1)
        mine = mine == me_p * local_count + local
        start = jnp.sum(jnp.where(mine, starts[t : t + 1, :], 0), axis=1, keepdims=True)
        length = jnp.sum(jnp.where(mine, lengths[t : t + 1, :], 0), axis=1, keepdims=True)
        hot = (row - band_row == start) & (band_row < length)
        hot = jnp.where(hot, 1.0, 0.0).astype(jnp.bfloat16)
        placed = jnp.dot(rwland[t, local], hot, preferred_element_type=jnp.float32)
        wide[local, t * slices : (t + 1) * slices, :] = placed.astype(jnp.bfloat16)

    dist = 2.0 * total_cols

    def step(s):
        c, local = lax.rem(s, chunks), lax.div(s, chunks)

        @pl.when(s + DEPTH < steps)
        def _():
            each_proj(lambda j: raw_copy(s + DEPTH, j, me_p).start())

        own_copy(s).wait()
        each_proj(lambda j: raw_copy(s, j, proj_peer(j)).wait_recv())

        def weigh(b):
            at = pl.ds(pl.multiple_of(b * 128, 128), 128)
            row = b * 128 + lax.broadcasted_iota(jnp.int32, (128, cw), 0)
            column = me_t * cols_dev + c * cw + lax.broadcasted_iota(jnp.int32, (128, cw), 1)
            v = row.astype(jnp.float32) + (0.5 - total_rows / 2.0)
            u = column.astype(jnp.float32) + (0.5 - total_cols / 2.0)
            weight = dist * lax.rsqrt(dist * dist + u * u + v * v)
            value = landing[c, local, at, :].astype(jnp.float32) * weight
            weighted[at, :] = value.astype(jnp.bfloat16)

        each(total_rows // 128, 0, weigh)

        y = jnp.dot(wide[local], weighted[...], preferred_element_type=jnp.float32)
        ybuf[s] = y.astype(jnp.bfloat16).reshape(n_tile, slices, cw)
        each_tile(lambda j: z_copy(s, j, me_t).start())
        column = pl.multiple_of(128 + me_t * cols_dev + c * cw, 128)
        zbuf[local, :, pl.ds(column, cw)] = ybuf[s, me_t]
        each_proj(lambda j: raw_copy(s, j, me_p).wait_send())

    def window(local):
        def arrived(s):
            each_tile(lambda j: z_copy(s, j, tile_source(j)).wait_recv())

        each((local + 1) * chunks, local * chunks, arrived)
        part = zbuf[local]
        offset = offsets[:, local : local + 1]
        bit = 1
        while 2 * bit <= (total_cols - win_cols) // 128:
            bit *= 2
        while bit:
            width = min(win_cols + 256 + 128 * (bit - 1), part.shape[1])
            moved = part[:, 128 * bit : 128 * bit + width]
            if moved.shape[1] < width:
                tail = jnp.zeros((slices, width - moved.shape[1]), part.dtype)
                moved = jnp.concatenate([moved, tail], axis=1)
            skip = jnp.broadcast_to(offset, (slices, width)) & bit
            part = jnp.where(skip != 0, moved, part[:, :width])
            bit //= 2
        for group in range(win_cols // 256):
            value = jnp.dot(
                part[:, 256 * group : 256 * group + 512],
                taps[...],
                preferred_element_type=jnp.float32,
            )
            filt[local, :, 256 * group : 256 * group + 256] = value.astype(jnp.bfloat16)

    def product(local, at):
        return jnp.dot(
            filt[local], cbuf[local, :, at : at + 256], preferred_element_type=jnp.float32
        )

    def add_up(local):
        window(local)
        c_copy(local).wait()
        for at in range(0, vt, 256):
            value = product(local, at)
            acc[:, at : at + 256] = value if local == 0 else acc[:, at : at + 256] + value

    done = 0
    for local in range(local_count):
        for t in range(n_tile):
            place(local, t)
        if local > 0:
            until = min(local * chunks + 2, steps)
            each(until, done, step)
            done = until
            add_up(local - 1)
        else:
            done = min(chunks - 1, 2)
            each(done, 0, step)
    each(steps, done, step)

    last = local_count - 1
    window(last)
    c_copy(last).wait()
    for n in range(PARTS):
        for half in range(part_cols // 256):
            at = n * part_cols + 256 * half
            value = product(last, at)
            if last > 0:
                value = value + acc[:, at : at + 256]
            psend[n, :, :, 256 * half : 256 * half + 256] = value.reshape(
                n_proj, slices // n_proj, 256
            ).astype(psend.dtype)
        each_proj(lambda j: p_copy(n, j, me_p).start())
        precv[n, me_p] = psend[n, me_p]

    each_tile(lambda j: rw_copy(j, me_t).wait_send())
    each_tile(lambda j: each(steps, 0, lambda s: z_copy(s, j, me_t).wait_send()))
    for n in range(PARTS):
        each_proj(lambda j: p_copy(n, j, proj_peer(j)).wait_recv())
        total = precv[n, 0].astype(jnp.float32)
        for source in range(1, n_proj):
            total = total + precv[n, source].astype(jnp.float32)
        out[:, n * part_cols : (n + 1) * part_cols] = total

    for n in range(PARTS):
        each_proj(lambda j: p_copy(n, j, me_p).wait_send())


def body(raw, row_weights, col_weights, band_start, band_length, col_offset):
    proj_count, rows_dev, cols_dev = raw.shape
    n_proj = lax.axis_size("proj")
    n_tile = lax.axis_size("tile")
    total_rows = rows_dev * n_proj
    total_cols = cols_dev * n_tile
    local_count, _, slices, lmax = row_weights.shape
    win_cols, vt = col_weights.shape[2:]
    cw = min(CHUNK, cols_dev)
    chunks = cols_dev // cw
    steps = local_count * chunks
    out_rows = slices // n_proj
    sum_type = jnp.bfloat16 if out_rows % 16 == 0 else jnp.float32
    bf16 = jnp.bfloat16
    vmem = pl.BlockSpec(memory_space=pltpu.VMEM)
    hbm = pl.BlockSpec(memory_space=pl.ANY)
    dma = pltpu.SemaphoreType.DMA
    flops = 2 * local_count * n_tile * slices * total_rows * cols_dev
    return pl.pallas_call(
        functools.partial(kernel, n_proj, n_tile, chunks, cw),
        out_shape=jax.ShapeDtypeStruct((out_rows, vt), jnp.float32),
        in_specs=[hbm] * 6,
        out_specs=vmem,
        scratch_shapes=[
            pltpu.VMEM((n_tile, proj_count), jnp.int32),
            pltpu.VMEM((n_tile, proj_count), jnp.int32),
            pltpu.VMEM((1, local_count), jnp.int32),
            pltpu.VMEM((512, 256), bf16),
            pltpu.VMEM((chunks, local_count, total_rows, cw), bf16),
            pltpu.VMEM((local_count, n_tile * slices, total_rows), bf16),
            pltpu.VMEM((total_rows, cw), bf16),
            pltpu.VMEM((steps, n_tile, slices, cw), bf16),
            pltpu.VMEM((local_count, slices, total_cols + 256), bf16),
            pltpu.VMEM((n_tile, local_count, slices, lmax), bf16),
            pltpu.VMEM((local_count, slices, win_cols), bf16),
            pltpu.VMEM((local_count, win_cols, vt), bf16),
            pltpu.VMEM((slices, vt), jnp.float32),
            pltpu.VMEM((PARTS, n_proj, out_rows, vt // PARTS), sum_type),
            pltpu.VMEM((PARTS, n_proj, out_rows, vt // PARTS), sum_type),
            dma((3,)),
            dma((steps,)),
            dma((steps, n_proj)),
            dma((steps, n_proj)),
            dma,
            dma((n_tile,)),
            dma((n_tile,)),
            dma((steps, n_tile)),
            dma((steps, n_tile)),
            dma((local_count,)),
            dma((PARTS, n_proj)),
            dma((PARTS, n_proj)),
        ],
        compiler_params=pltpu.CompilerParams(
            collective_id=0, has_side_effects=True, vmem_limit_bytes=VMEM_BYTES
        ),
        cost_estimate=pl.CostEstimate(
            flops=flops, bytes_accessed=16 * 1024 * 1024, transcendentals=0
        ),
    )(band_start.T, band_length.T, col_offset.T, row_weights, raw, col_weights)


def solution(mesh):
    return jax.shard_map(
        body,
        mesh=mesh,
        in_specs=(
            P(None, "proj", "tile"),
            P("proj", "tile", None, None),
            P("proj", "tile", None, None),
            P(),
            P(),
            P("proj", "tile"),
        ),
        out_specs=P("proj", "tile"),
        check_vma=False,
    )
```

```python
import functools
import math

import jax
import jax.numpy as jnp
from jax import lax
from jax.experimental import pallas as pl
from jax.experimental.pallas import tpu as pltpu
from jax.sharding import PartitionSpec as P

MESH = pl.DeviceIdType.MESH
CHUNK = 128
PARTS = 4
DEPTH = 6
VMEM_BYTES = 63 * 1024 * 1024


def tap_matrix():
    row = lax.broadcasted_iota(jnp.int32, (512, 256), 0)
    n = lax.broadcasted_iota(jnp.int32, (512, 256), 1) - row + 128
    n_f = n.astype(jnp.float32)
    safe_sq = jnp.where(n == 0, 1.0, n_f * n_f)
    odd = jnp.where((n & 1) != 0, -1.0 / (math.pi * math.pi * safe_sq), 0.0)
    value = jnp.where(n == 0, 0.25, odd)
    value = jnp.where((n >= -128) & (n <= 127), value, 0.0)
    return value.astype(jnp.bfloat16)


def kernel(
    n_proj, n_tile, chunks, cw,
    starts_in, lengths_in, offsets_in, rw, raw, col_w, out,
    starts, lengths, offsets, taps,
    landing, wide, weighted, ybuf, zbuf, rwland, filt, cbuf, acc, psend, precv,
    int_sem, own_sem, raw_send, raw_recv, rw_own, rw_send, rw_recv, z_send, z_recv,
    c_sem, p_send, p_recv,
):
    me_p = lax.axis_index("proj")
    me_t = lax.axis_index("tile")
    local_count = landing.shape[1]
    total_rows = landing.shape[2]
    rows_dev = total_rows // n_proj
    cols_dev = chunks * cw
    total_cols = cols_dev * n_tile
    slices, lmax = rw.shape[2], rw.shape[3]
    win_cols = col_w.shape[2]
    vt = col_w.shape[3]
    part_cols = vt // PARTS
    steps = local_count * chunks

    core = lax.rem(me_p, 2)
    bits, bit = [], 1
    while bit < n_proj:
        bits.append(bit * (1 - 2 * lax.rem(lax.div(me_p, bit), 2)))
        bit *= 2

    def flipped(mask):
        return sum(((mask >> i) & 1) * step for i, step in enumerate(bits))

    proj_peers = {}
    for j in [*range(2, n_proj, 2), *range(n_proj - 1, 0, -2)]:
        other = (j & ~6) | ((j & 2) << 1) | ((j & 4) >> 1) if j % 2 == 0 and n_proj > 4 else j
        proj_peers[j] = me_p + flipped(j) + core * (flipped(other) - flipped(j))
    tile_peers = {j: lax.rem(me_t + j, n_tile) for j in range(1, n_tile)}
    tile_sources = {j: lax.rem(me_t + n_tile - j, n_tile) for j in range(1, n_tile)}

    def proj_peer(j):
        return proj_peers[j]

    def tile_peer(j):
        return tile_peers[j]

    def tile_source(j):
        return tile_sources[j]

    def c_copy(local):
        return pltpu.make_async_copy(col_w.at[local, 0], cbuf.at[local], c_sem.at[local])

    def raw_place(s, row_block):
        rows = pl.ds(pl.multiple_of(row_block * rows_dev, rows_dev), rows_dev)
        return landing.at[lax.rem(s, chunks), lax.div(s, chunks), rows]

    def raw_piece(s, peer):
        columns = pl.ds(pl.multiple_of(lax.rem(s, chunks) * cw, cw), cw)
        return raw.at[peer * local_count + lax.div(s, chunks), :, columns]

    def own_copy(s):
        return pltpu.make_async_copy(raw_piece(s, me_p), raw_place(s, me_p), own_sem.at[s])

    def raw_copy(s, j, row_block):
        peer = proj_peer(j)
        return pltpu.make_async_remote_copy(
            src_ref=raw_piece(s, peer),
            dst_ref=raw_place(s, row_block),
            send_sem=raw_send.at[s, j],
            recv_sem=raw_recv.at[s, j],
            device_id=(peer, me_t),
            device_id_type=MESH,
        )

    def rw_copy(j, slot):
        return pltpu.make_async_remote_copy(
            src_ref=rw.at[:, 0],
            dst_ref=rwland.at[slot],
            send_sem=rw_send.at[j],
            recv_sem=rw_recv.at[j],
            device_id=(me_p, tile_peer(j)),
            device_id_type=MESH,
        )

    def z_place(s, tile):
        column = pl.multiple_of(128 + tile * cols_dev + lax.rem(s, chunks) * cw, 128)
        return zbuf.at[lax.div(s, chunks), :, pl.ds(column, cw)]

    def z_copy(s, j, tile):
        return pltpu.make_async_remote_copy(
            src_ref=ybuf.at[s, tile_peer(j)],
            dst_ref=z_place(s, tile),
            send_sem=z_send.at[s, j],
            recv_sem=z_recv.at[s, j],
            device_id=(me_p, tile_peer(j)),
            device_id_type=MESH,
        )

    def p_copy(n, j, slot):
        return pltpu.make_async_remote_copy(
            src_ref=psend.at[n, proj_peer(j)],
            dst_ref=precv.at[n, slot],
            send_sem=p_send.at[n, j],
            recv_sem=p_recv.at[n, j],
            device_id=(proj_peer(j), me_t),
            device_id_type=MESH,
        )

    def each(count, first, f):
        def step(i, carry):
            f(i)
            return carry

        lax.fori_loop(first, count, step, 0)

    def each_proj(f):
        for j in proj_peers:
            f(j)

    def each_tile(f):
        for j in tile_peers:
            f(j)

    barrier = pltpu.get_barrier_semaphore()

    def greet_proj(j):
        pl.semaphore_signal(barrier, inc=1, device_id=(proj_peer(j), me_t), device_id_type=MESH)

    def greet_tile(j):
        pl.semaphore_signal(barrier, inc=1, device_id=(me_p, tile_peer(j)), device_id_type=MESH)

    each_proj(greet_proj)
    each_tile(greet_tile)

    small = [
        pltpu.make_async_copy(starts_in, starts, int_sem.at[0]),
        pltpu.make_async_copy(lengths_in, lengths, int_sem.at[1]),
        pltpu.make_async_copy(offsets_in, offsets, int_sem.at[2]),
        pltpu.make_async_copy(rw.at[:, 0], rwland.at[me_t], rw_own),
    ]
    for copy in small:
        copy.start()
    each(steps, 0, lambda s: own_copy(s).start())
    edge = jnp.zeros((local_count, slices, 128), zbuf.dtype)
    zbuf[:, :, 0:128] = edge
    zbuf[:, :, 128 + total_cols :] = edge

    pl.semaphore_wait(barrier, n_proj + n_tile - 2)

    each_tile(lambda j: rw_copy(j, me_t).start())
    for s in range(min(DEPTH, steps)):
        each_proj(lambda j: raw_copy(s, j, me_p).start())
    for local in range(local_count):
        c_copy(local).start()
    taps[...] = tap_matrix()
    for copy in small:
        copy.wait()
    each_tile(lambda j: rw_copy(j, tile_source(j)).wait_recv())

    def place(local, t):
        band_row = lax.broadcasted_iota(jnp.int32, (lmax, total_rows), 0)
        row = lax.broadcasted_iota(jnp.int32, (lmax, total_rows), 1)
        mine = lax.broadcasted_iota(jnp.int32, (1, starts.shape[1]), 1)
        mine = mine == me_p * local_count + local
        start = jnp.sum(jnp.where(mine, starts[t : t + 1, :], 0), axis=1, keepdims=True)
        length = jnp.sum(jnp.where(mine, lengths[t : t + 1, :], 0), axis=1, keepdims=True)
        hot = (row - band_row == start) & (band_row < length)
        hot = jnp.where(hot, 1.0, 0.0).astype(jnp.bfloat16)
        placed = jnp.dot(rwland[t, local], hot, preferred_element_type=jnp.float32)
        wide[local, t * slices : (t + 1) * slices, :] = placed.astype(jnp.bfloat16)

    dist = 2.0 * total_cols

    def step(s):
        c, local = lax.rem(s, chunks), lax.div(s, chunks)

        @pl.when(s + DEPTH < steps)
        def _():
            each_proj(lambda j: raw_copy(s + DEPTH, j, me_p).start())

        own_copy(s).wait()
        each_proj(lambda j: raw_copy(s, j, proj_peer(j)).wait_recv())

        def weigh(b):
            at = pl.ds(pl.multiple_of(b * 128, 128), 128)
            row = b * 128 + lax.broadcasted_iota(jnp.int32, (128, cw), 0)
            column = me_t * cols_dev + c * cw + lax.broadcasted_iota(jnp.int32, (128, cw), 1)
            v = row.astype(jnp.float32) + (0.5 - total_rows / 2.0)
            u = column.astype(jnp.float32) + (0.5 - total_cols / 2.0)
            weight = dist * lax.rsqrt(dist * dist + u * u + v * v)
            value = landing[c, local, at, :].astype(jnp.float32) * weight
            weighted[at, :] = value.astype(jnp.bfloat16)

        each(total_rows // 128, 0, weigh)

        y = jnp.dot(wide[local], weighted[...], preferred_element_type=jnp.float32)
        ybuf[s] = y.astype(jnp.bfloat16).reshape(n_tile, slices, cw)
        each_tile(lambda j: z_copy(s, j, me_t).start())
        column = pl.multiple_of(128 + me_t * cols_dev + c * cw, 128)
        zbuf[local, :, pl.ds(column, cw)] = ybuf[s, me_t]
        each_proj(lambda j: raw_copy(s, j, me_p).wait_send())

    def window(local):
        def arrived(s):
            each_tile(lambda j: z_copy(s, j, tile_source(j)).wait_recv())

        each((local + 1) * chunks, local * chunks, arrived)
        part = zbuf[local]
        offset = offsets[:, local : local + 1]
        bit = 1
        while 2 * bit <= (total_cols - win_cols) // 128:
            bit *= 2
        while bit:
            width = min(win_cols + 256 + 128 * (bit - 1), part.shape[1])
            moved = part[:, 128 * bit : 128 * bit + width]
            if moved.shape[1] < width:
                tail = jnp.zeros((slices, width - moved.shape[1]), part.dtype)
                moved = jnp.concatenate([moved, tail], axis=1)
            skip = jnp.broadcast_to(offset, (slices, width)) & bit
            part = jnp.where(skip != 0, moved, part[:, :width])
            bit //= 2
        for group in range(win_cols // 256):
            value = jnp.dot(
                part[:, 256 * group : 256 * group + 512],
                taps[...],
                preferred_element_type=jnp.float32,
            )
            filt[local, :, 256 * group : 256 * group + 256] = value.astype(jnp.bfloat16)

    def product(local, at):
        return jnp.dot(
            filt[local], cbuf[local, :, at : at + 256], preferred_element_type=jnp.float32
        )

    def add_up(local):
        window(local)
        c_copy(local).wait()
        for at in range(0, vt, 256):
            value = product(local, at)
            acc[:, at : at + 256] = value if local == 0 else acc[:, at : at + 256] + value

    done = 0
    for local in range(local_count):
        for t in range(n_tile):
            place(local, t)
        if local > 0:
            until = min(local * chunks + (chunks + 1) // 2, steps)
            each(until, done, step)
            done = until
            add_up(local - 1)
        else:
            done = min(chunks - 1, 2)
            each(done, 0, step)
    each(steps, done, step)

    last = local_count - 1
    window(last)
    c_copy(last).wait()
    for n in range(PARTS):
        for half in range(part_cols // 256):
            at = n * part_cols + 256 * half
            value = product(last, at)
            if last > 0:
                value = value + acc[:, at : at + 256]
            psend[n, :, :, 256 * half : 256 * half + 256] = value.reshape(
                n_proj, slices // n_proj, 256
            ).astype(psend.dtype)
        each_proj(lambda j: p_copy(n, j, me_p).start())
        precv[n, me_p] = psend[n, me_p]

    each_tile(lambda j: rw_copy(j, me_t).wait_send())
    each_tile(lambda j: each(steps, 0, lambda s: z_copy(s, j, me_t).wait_send()))
    for n in range(PARTS):
        each_proj(lambda j: p_copy(n, j, proj_peer(j)).wait_recv())
        total = precv[n, 0].astype(jnp.float32)
        for source in range(1, n_proj):
            total = total + precv[n, source].astype(jnp.float32)
        out[:, n * part_cols : (n + 1) * part_cols] = total

    for n in range(PARTS):
        each_proj(lambda j: p_copy(n, j, me_p).wait_send())


def body(raw, row_weights, col_weights, band_start, band_length, col_offset):
    proj_count, rows_dev, cols_dev = raw.shape
    n_proj = lax.axis_size("proj")
    n_tile = lax.axis_size("tile")
    total_rows = rows_dev * n_proj
    total_cols = cols_dev * n_tile
    local_count, _, slices, lmax = row_weights.shape
    win_cols, vt = col_weights.shape[2:]
    cw = min(CHUNK, cols_dev)
    chunks = cols_dev // cw
    steps = local_count * chunks
    out_rows = slices // n_proj
    sum_type = jnp.bfloat16 if out_rows % 16 == 0 else jnp.float32
    bf16 = jnp.bfloat16
    vmem = pl.BlockSpec(memory_space=pltpu.VMEM)
    hbm = pl.BlockSpec(memory_space=pl.ANY)
    dma = pltpu.SemaphoreType.DMA
    flops = 2 * local_count * n_tile * slices * total_rows * cols_dev
    return pl.pallas_call(
        functools.partial(kernel, n_proj, n_tile, chunks, cw),
        out_shape=jax.ShapeDtypeStruct((out_rows, vt), jnp.float32),
        in_specs=[hbm] * 6,
        out_specs=vmem,
        scratch_shapes=[
            pltpu.VMEM((n_tile, proj_count), jnp.int32),
            pltpu.VMEM((n_tile, proj_count), jnp.int32),
            pltpu.VMEM((1, local_count), jnp.int32),
            pltpu.VMEM((512, 256), bf16),
            pltpu.VMEM((chunks, local_count, total_rows, cw), bf16),
            pltpu.VMEM((local_count, n_tile * slices, total_rows), bf16),
            pltpu.VMEM((total_rows, cw), bf16),
            pltpu.VMEM((steps, n_tile, slices, cw), bf16),
            pltpu.VMEM((local_count, slices, total_cols + 256), bf16),
            pltpu.VMEM((n_tile, local_count, slices, lmax), bf16),
            pltpu.VMEM((local_count, slices, win_cols), bf16),
            pltpu.VMEM((local_count, win_cols, vt), bf16),
            pltpu.VMEM((slices, vt), jnp.float32),
            pltpu.VMEM((PARTS, n_proj, out_rows, vt // PARTS), sum_type),
            pltpu.VMEM((PARTS, n_proj, out_rows, vt // PARTS), sum_type),
            dma((3,)),
            dma((steps,)),
            dma((steps, n_proj)),
            dma((steps, n_proj)),
            dma,
            dma((n_tile,)),
            dma((n_tile,)),
            dma((steps, n_tile)),
            dma((steps, n_tile)),
            dma((local_count,)),
            dma((PARTS, n_proj)),
            dma((PARTS, n_proj)),
        ],
        compiler_params=pltpu.CompilerParams(
            collective_id=0, has_side_effects=True, vmem_limit_bytes=VMEM_BYTES
        ),
        cost_estimate=pl.CostEstimate(
            flops=flops, bytes_accessed=16 * 1024 * 1024, transcendentals=0
        ),
    )(band_start.T, band_length.T, col_offset.T, row_weights, raw, col_weights)


def solution(mesh):
    return jax.shard_map(
        body,
        mesh=mesh,
        in_specs=(
            P(None, "proj", "tile"),
            P("proj", "tile", None, None),
            P("proj", "tile", None, None),
            P(),
            P(),
            P("proj", "tile"),
        ),
        out_specs=P("proj", "tile"),
        check_vma=False,
    )
```

```python
import functools
import math

import jax
import jax.numpy as jnp
from jax import lax
from jax.experimental import pallas as pl
from jax.experimental.pallas import tpu as pltpu
from jax.sharding import PartitionSpec as P

MESH = pl.DeviceIdType.MESH
CHUNK = 256
PARTS = 4
DEPTH = 3
VMEM_BYTES = 63 * 1024 * 1024


def tap_matrix():
    row = lax.broadcasted_iota(jnp.int32, (512, 256), 0)
    n = lax.broadcasted_iota(jnp.int32, (512, 256), 1) - row + 128
    n_f = n.astype(jnp.float32)
    safe_sq = jnp.where(n == 0, 1.0, n_f * n_f)
    odd = jnp.where((n & 1) != 0, -1.0 / (math.pi * math.pi * safe_sq), 0.0)
    value = jnp.where(n == 0, 0.25, odd)
    value = jnp.where((n >= -128) & (n <= 127), value, 0.0)
    return value.astype(jnp.bfloat16)


def kernel(
    n_proj, n_tile, chunks, cw,
    starts_in, lengths_in, offsets_in, rw, raw, col_w, out,
    starts, lengths, offsets, taps,
    landing, wide, weighted, ybuf, zbuf, rwland, filt, cbuf, acc, psend, precv,
    int_sem, own_sem, raw_send, raw_recv, rw_own, rw_send, rw_recv, z_send, z_recv,
    c_sem, p_send, p_recv,
):
    me_p = lax.axis_index("proj")
    me_t = lax.axis_index("tile")
    local_count = landing.shape[1]
    total_rows = landing.shape[2]
    rows_dev = total_rows // n_proj
    cols_dev = chunks * cw
    total_cols = cols_dev * n_tile
    slices, lmax = rw.shape[2], rw.shape[3]
    win_cols = col_w.shape[2]
    vt = col_w.shape[3]
    part_cols = vt // PARTS
    steps = local_count * chunks

    core = lax.rem(me_p, 2)
    bits, bit = [], 1
    while bit < n_proj:
        bits.append(bit * (1 - 2 * lax.rem(lax.div(me_p, bit), 2)))
        bit *= 2

    def flipped(mask):
        return sum(((mask >> i) & 1) * step for i, step in enumerate(bits))

    proj_peers = {}
    for j in [*range(2, n_proj, 2), *range(n_proj - 1, 0, -2)]:
        other = (j & ~6) | ((j & 2) << 1) | ((j & 4) >> 1) if j % 2 == 0 and n_proj > 4 else j
        proj_peers[j] = me_p + flipped(j) + core * (flipped(other) - flipped(j))
    tile_peers = {j: lax.rem(me_t + j, n_tile) for j in range(1, n_tile)}
    tile_sources = {j: lax.rem(me_t + n_tile - j, n_tile) for j in range(1, n_tile)}

    def proj_peer(j):
        return proj_peers[j]

    def tile_peer(j):
        return tile_peers[j]

    def tile_source(j):
        return tile_sources[j]

    def c_copy(local):
        return pltpu.make_async_copy(col_w.at[local, 0], cbuf.at[local], c_sem.at[local])

    def raw_place(s, row_block):
        rows = pl.ds(pl.multiple_of(row_block * rows_dev, rows_dev), rows_dev)
        return landing.at[lax.rem(s, chunks), lax.div(s, chunks), rows]

    def raw_piece(s, peer):
        columns = pl.ds(pl.multiple_of(lax.rem(s, chunks) * cw, cw), cw)
        return raw.at[peer * local_count + lax.div(s, chunks), :, columns]

    def own_copy(s):
        return pltpu.make_async_copy(raw_piece(s, me_p), raw_place(s, me_p), own_sem.at[s])

    def raw_copy(s, j, row_block):
        peer = proj_peer(j)
        return pltpu.make_async_remote_copy(
            src_ref=raw_piece(s, peer),
            dst_ref=raw_place(s, row_block),
            send_sem=raw_send.at[s, j],
            recv_sem=raw_recv.at[s, j],
            device_id=(peer, me_t),
            device_id_type=MESH,
        )

    def rw_copy(j, slot):
        return pltpu.make_async_remote_copy(
            src_ref=rw.at[:, 0],
            dst_ref=rwland.at[slot],
            send_sem=rw_send.at[j],
            recv_sem=rw_recv.at[j],
            device_id=(me_p, tile_peer(j)),
            device_id_type=MESH,
        )

    def z_place(s, tile):
        column = pl.multiple_of(128 + tile * cols_dev + lax.rem(s, chunks) * cw, 128)
        return zbuf.at[lax.div(s, chunks), :, pl.ds(column, cw)]

    def z_copy(s, j, tile):
        return pltpu.make_async_remote_copy(
            src_ref=ybuf.at[s, tile_peer(j)],
            dst_ref=z_place(s, tile),
            send_sem=z_send.at[s, j],
            recv_sem=z_recv.at[s, j],
            device_id=(me_p, tile_peer(j)),
            device_id_type=MESH,
        )

    def p_copy(n, j, slot):
        return pltpu.make_async_remote_copy(
            src_ref=psend.at[n, proj_peer(j)],
            dst_ref=precv.at[n, slot],
            send_sem=p_send.at[n, j],
            recv_sem=p_recv.at[n, j],
            device_id=(proj_peer(j), me_t),
            device_id_type=MESH,
        )

    def each(count, first, f):
        def step(i, carry):
            f(i)
            return carry

        lax.fori_loop(first, count, step, 0)

    def each_proj(f):
        for j in proj_peers:
            f(j)

    def each_tile(f):
        for j in tile_peers:
            f(j)

    barrier = pltpu.get_barrier_semaphore()

    def greet_proj(j):
        pl.semaphore_signal(barrier, inc=1, device_id=(proj_peer(j), me_t), device_id_type=MESH)

    def greet_tile(j):
        pl.semaphore_signal(barrier, inc=1, device_id=(me_p, tile_peer(j)), device_id_type=MESH)

    each_proj(greet_proj)
    each_tile(greet_tile)

    small = [
        pltpu.make_async_copy(starts_in, starts, int_sem.at[0]),
        pltpu.make_async_copy(lengths_in, lengths, int_sem.at[1]),
        pltpu.make_async_copy(offsets_in, offsets, int_sem.at[2]),
        pltpu.make_async_copy(rw.at[:, 0], rwland.at[me_t], rw_own),
    ]
    for copy in small:
        copy.start()
    each(steps, 0, lambda s: own_copy(s).start())
    edge = jnp.zeros((local_count, slices, 128), zbuf.dtype)
    zbuf[:, :, 0:128] = edge
    zbuf[:, :, 128 + total_cols :] = edge

    pl.semaphore_wait(barrier, n_proj + n_tile - 2)

    each_tile(lambda j: rw_copy(j, me_t).start())
    for s in range(min(DEPTH, steps)):
        each_proj(lambda j: raw_copy(s, j, me_p).start())
    for local in range(local_count):
        c_copy(local).start()
    taps[...] = tap_matrix()
    for copy in small:
        copy.wait()
    each_tile(lambda j: rw_copy(j, tile_source(j)).wait_recv())

    def place(local, t):
        band_row = lax.broadcasted_iota(jnp.int32, (lmax, total_rows), 0)
        row = lax.broadcasted_iota(jnp.int32, (lmax, total_rows), 1)
        mine = lax.broadcasted_iota(jnp.int32, (1, starts.shape[1]), 1)
        mine = mine == me_p * local_count + local
        start = jnp.sum(jnp.where(mine, starts[t : t + 1, :], 0), axis=1, keepdims=True)
        length = jnp.sum(jnp.where(mine, lengths[t : t + 1, :], 0), axis=1, keepdims=True)
        hot = (row - band_row == start) & (band_row < length)
        hot = jnp.where(hot, 1.0, 0.0).astype(jnp.bfloat16)
        placed = jnp.dot(rwland[t, local], hot, preferred_element_type=jnp.float32)
        wide[local, t * slices : (t + 1) * slices, :] = placed.astype(jnp.bfloat16)

    dist = 2.0 * total_cols

    def step(s):
        c, local = lax.rem(s, chunks), lax.div(s, chunks)

        @pl.when(s + DEPTH < steps)
        def _():
            each_proj(lambda j: raw_copy(s + DEPTH, j, me_p).start())

        def weigh(source):
            at = pl.ds(pl.multiple_of(source * rows_dev, rows_dev), rows_dev)
            row = source * rows_dev + lax.broadcasted_iota(jnp.int32, (rows_dev, cw), 0)
            column = me_t * cols_dev + c * cw + lax.broadcasted_iota(jnp.int32, (rows_dev, cw), 1)
            v = row.astype(jnp.float32) + (0.5 - total_rows / 2.0)
            u = column.astype(jnp.float32) + (0.5 - total_cols / 2.0)
            weight = dist * lax.rsqrt(dist * dist + u * u + v * v)
            value = landing[c, local, at, :].astype(jnp.float32) * weight
            weighted[at, :] = value.astype(jnp.bfloat16)

        own_copy(s).wait()
        weigh(me_p)
        for j in proj_peers:
            raw_copy(s, j, proj_peer(j)).wait_recv()
            weigh(proj_peer(j))

        y = jnp.dot(wide[local], weighted[...], preferred_element_type=jnp.float32)
        ybuf[s] = y.astype(jnp.bfloat16).reshape(n_tile, slices, cw)
        each_tile(lambda j: z_copy(s, j, me_t).start())
        column = pl.multiple_of(128 + me_t * cols_dev + c * cw, 128)
        zbuf[local, :, pl.ds(column, cw)] = ybuf[s, me_t]
        each_proj(lambda j: raw_copy(s, j, me_p).wait_send())

    def window(local):
        def arrived(s):
            each_tile(lambda j: z_copy(s, j, tile_source(j)).wait_recv())

        each((local + 1) * chunks, local * chunks, arrived)
        part = zbuf[local]
        offset = offsets[:, local : local + 1]
        bit = 1
        while 2 * bit <= (total_cols - win_cols) // 128:
            bit *= 2
        while bit:
            width = min(win_cols + 256 + 128 * (bit - 1), part.shape[1])
            moved = part[:, 128 * bit : 128 * bit + width]
            if moved.shape[1] < width:
                tail = jnp.zeros((slices, width - moved.shape[1]), part.dtype)
                moved = jnp.concatenate([moved, tail], axis=1)
            skip = jnp.broadcast_to(offset, (slices, width)) & bit
            part = jnp.where(skip != 0, moved, part[:, :width])
            bit //= 2
        for group in range(win_cols // 256):
            value = jnp.dot(
                part[:, 256 * group : 256 * group + 512],
                taps[...],
                preferred_element_type=jnp.float32,
            )
            filt[local, :, 256 * group : 256 * group + 256] = value.astype(jnp.bfloat16)

    def product(local, at):
        return jnp.dot(
            filt[local], cbuf[local, :, at : at + 256], preferred_element_type=jnp.float32
        )

    def add_up(local):
        window(local)
        c_copy(local).wait()
        for at in range(0, vt, 256):
            value = product(local, at)
            acc[:, at : at + 256] = value if local == 0 else acc[:, at : at + 256] + value

    done = 0
    for local in range(local_count):
        for t in range(n_tile):
            place(local, t)
        if local > 0:
            until = min(local * chunks + 2, steps)
            each(until, done, step)
            done = until
            add_up(local - 1)
        else:
            done = min(chunks - 1, 2)
            each(done, 0, step)
    each(steps, done, step)

    last = local_count - 1
    window(last)
    c_copy(last).wait()
    for n in range(PARTS):
        for half in range(part_cols // 256):
            at = n * part_cols + 256 * half
            value = product(last, at)
            if last > 0:
                value = value + acc[:, at : at + 256]
            psend[n, :, :, 256 * half : 256 * half + 256] = value.reshape(
                n_proj, slices // n_proj, 256
            ).astype(psend.dtype)
        each_proj(lambda j: p_copy(n, j, me_p).start())
        precv[n, me_p] = psend[n, me_p]

    each_tile(lambda j: rw_copy(j, me_t).wait_send())
    each_tile(lambda j: each(steps, 0, lambda s: z_copy(s, j, me_t).wait_send()))
    for n in range(PARTS):
        each_proj(lambda j: p_copy(n, j, proj_peer(j)).wait_recv())
        total = precv[n, 0].astype(jnp.float32)
        for source in range(1, n_proj):
            total = total + precv[n, source].astype(jnp.float32)
        out[:, n * part_cols : (n + 1) * part_cols] = total

    for n in range(PARTS):
        each_proj(lambda j: p_copy(n, j, me_p).wait_send())


def body(raw, row_weights, col_weights, band_start, band_length, col_offset):
    proj_count, rows_dev, cols_dev = raw.shape
    n_proj = lax.axis_size("proj")
    n_tile = lax.axis_size("tile")
    total_rows = rows_dev * n_proj
    total_cols = cols_dev * n_tile
    local_count, _, slices, lmax = row_weights.shape
    win_cols, vt = col_weights.shape[2:]
    cw = min(CHUNK, cols_dev)
    chunks = cols_dev // cw
    steps = local_count * chunks
    out_rows = slices // n_proj
    sum_type = jnp.bfloat16 if out_rows % 16 == 0 else jnp.float32
    bf16 = jnp.bfloat16
    vmem = pl.BlockSpec(memory_space=pltpu.VMEM)
    hbm = pl.BlockSpec(memory_space=pl.ANY)
    dma = pltpu.SemaphoreType.DMA
    flops = 2 * local_count * n_tile * slices * total_rows * cols_dev
    return pl.pallas_call(
        functools.partial(kernel, n_proj, n_tile, chunks, cw),
        out_shape=jax.ShapeDtypeStruct((out_rows, vt), jnp.float32),
        in_specs=[hbm] * 6,
        out_specs=vmem,
        scratch_shapes=[
            pltpu.VMEM((n_tile, proj_count), jnp.int32),
            pltpu.VMEM((n_tile, proj_count), jnp.int32),
            pltpu.VMEM((1, local_count), jnp.int32),
            pltpu.VMEM((512, 256), bf16),
            pltpu.VMEM((chunks, local_count, total_rows, cw), bf16),
            pltpu.VMEM((local_count, n_tile * slices, total_rows), bf16),
            pltpu.VMEM((total_rows, cw), bf16),
            pltpu.VMEM((steps, n_tile, slices, cw), bf16),
            pltpu.VMEM((local_count, slices, total_cols + 256), bf16),
            pltpu.VMEM((n_tile, local_count, slices, lmax), bf16),
            pltpu.VMEM((local_count, slices, win_cols), bf16),
            pltpu.VMEM((local_count, win_cols, vt), bf16),
            pltpu.VMEM((slices, vt), jnp.float32),
            pltpu.VMEM((PARTS, n_proj, out_rows, vt // PARTS), sum_type),
            pltpu.VMEM((PARTS, n_proj, out_rows, vt // PARTS), sum_type),
            dma((3,)),
            dma((steps,)),
            dma((steps, n_proj)),
            dma((steps, n_proj)),
            dma,
            dma((n_tile,)),
            dma((n_tile,)),
            dma((steps, n_tile)),
            dma((steps, n_tile)),
            dma((local_count,)),
            dma((PARTS, n_proj)),
            dma((PARTS, n_proj)),
        ],
        compiler_params=pltpu.CompilerParams(
            collective_id=0, has_side_effects=True, vmem_limit_bytes=VMEM_BYTES
        ),
        cost_estimate=pl.CostEstimate(
            flops=flops, bytes_accessed=16 * 1024 * 1024, transcendentals=0
        ),
    )(band_start.T, band_length.T, col_offset.T, row_weights, raw, col_weights)


def solution(mesh):
    return jax.shard_map(
        body,
        mesh=mesh,
        in_specs=(
            P(None, "proj", "tile"),
            P("proj", "tile", None, None),
            P("proj", "tile", None, None),
            P(),
            P(),
            P("proj", "tile"),
        ),
        out_specs=P("proj", "tile"),
        check_vma=False,
    )
```
